512 devices in a mesh: ctx: 64 (over z_hi, y, core), exp: 8 (over x, z_lo).
Axes of the slice: x: 4, y: 8, z: 8 (z_hi: 4, z_lo: 2; z = z_hi * 2 + z_lo), core: 2. Of those that a mesh axis runs over, the one named last changes fastest.
Arguments:
- residual: bfloat16 [65536, 2048], P(('ctx', 'exp')), may hold values from -6 to 6
- out_grad: bfloat16 [65536, 2048], P(('ctx', 'exp')), may hold values from -6 to 6
- norm_gain: bfloat16 [2048], replicated, may hold values from 0.25 to 1.75
- expert_ids: int32 [65536, 6], P(('ctx', 'exp')), may hold values from 0 to 63, as said below
- route_weights: bfloat16 [65536, 6], P(('ctx', 'exp')), may hold values from 0.19921875 to 1
- gate_up: bfloat16 [8, 2, 2048, 768], P('exp', None, 'ctx'), may hold values from -0.125 to 0.125
- down_proj: bfloat16 [8, 768, 2048], P('exp', 'ctx'), may hold values from -0.21875 to 0.21875
- out_proj: bfloat16 [1024, 2048], P('exp'), may hold values from -0.1875 to 0.1875
- queries: bfloat16 [65536, 1536], P('ctx', 'exp'), may hold values from -14 to 14
- keys_in: bfloat16 [65536, 1536], P('ctx', 'exp'), may hold values from -6 to 6
- values_in: bfloat16 [65536, 1024], P('ctx', 'exp'), may hold values from -6 to 6
- segments: int32 [65536], P('ctx'), may hold values from 0 to 255, never falling along the last dimension, each value on 1 to 512 neighbouring positions
Outputs:
- residual_grad: bfloat16 [65536, 2048], P(('ctx', 'exp'))
- query_grad: bfloat16 [65536, 1536], P('ctx', 'exp')
- key_grad: bfloat16 [65536, 1536], P('ctx', 'exp')
- value_grad: bfloat16 [65536, 1024], P('ctx', 'exp')
The draws below stay inside these ranges and needn't reach their ends.
Inputs may be any that keep to these rules, and one draw needn't show every extreme that they name: `expert_ids`: each token names 6 different experts, exactly one of them below 8. Among the 128 tokens of one device at most 24 name any one expert below 8. `segments`: tokens of one document are consecutive; a document has at most 512 tokens.
All inputs are finite; a program needn't handle non-finite values.
Results may differ from the reference program's by a relative error of at most 0.029.
Values may be sent and summed in bfloat16 or wider, within the bound.
A program may use at most 128 MiB of HBM per device.

```python
import math
import jax
import jax.numpy as jnp
import numpy as np
from jax import lax

D = 2048
HEADS = 8
QK = 192
VD = 128
FF = 768
EXPERTS = 64
TOPK = 6
TOK_CTX = 1024
REACH = 512
SEQ = 65536
TOK_DEV = 128
CAP = 24
N_CTX = 64
N_EXP = 8


def key_field(key):
    normal_part = jax.random.truncated_normal(key, -6.0, 6.0, (SEQ, HEADS * QK), jnp.float32)
    return normal_part


def draw_queries(key, part):
    key = jax.random.fold_in(key, 5)
    values = jax.random.truncated_normal(key, -6.0, 6.0, (SEQ, HEADS * QK), jnp.float32)
    return values.astype(jnp.bfloat16)


def draw_keys_in(key, part):
    return key_field(key).astype(jnp.bfloat16)


def draw_expert_ids(key, part):
    key = jax.random.fold_in(key, 11)
    hot_key, order_key, dead_key, turn_key = jax.random.split(key, 4)
    tok_dev = TOK_CTX // N_EXP
    capacity = 3 * tok_dev // (2 * N_EXP)
    blocks = SEQ // tok_dev
    hot = jax.random.randint(hot_key, (N_CTX, 1), 0, N_EXP)
    hot_rows = jnp.broadcast_to(hot, (N_CTX, TOK_CTX)).reshape(blocks, tok_dev)
    scores = jax.random.randint(order_key, (blocks, tok_dev), 0, 1 << 16) * tok_dev + jnp.arange(tok_dev, dtype=jnp.int32)[None, :]
    ranks = jnp.argsort(jnp.argsort(scores, axis=1), axis=1).astype(jnp.int32)
    others = (hot_rows + 1 + (ranks - capacity) % (N_EXP - 1)) % N_EXP
    live = jnp.where(ranks < capacity, hot_rows, others).reshape(SEQ, 1)
    spare = EXPERTS - N_EXP
    start = jax.random.randint(dead_key, (SEQ, 1), 0, spare)
    dead = N_EXP + (start + jnp.arange(1, TOPK, dtype=jnp.int32)[None, :]) % spare
    chosen = jnp.concatenate([live, dead], axis=1)
    turn = jax.random.randint(turn_key, (SEQ, 1), 0, TOPK)
    where_from = (jnp.arange(TOPK, dtype=jnp.int32)[None, :] + turn) % TOPK
    return jnp.take_along_axis(chosen, where_from, axis=1).astype(jnp.int32)


def block_levels(stream_key, dims, cuts, least, top_value):
    def one(position, parts):
        draws = jax.random.uniform(jax.random.fold_in(jax.random.fold_in(stream_key, 6), position), (parts,), jnp.float32, least / len(cuts), top_value / len(cuts))
        return jnp.repeat(jnp.exp(draws), dims[position] // parts).reshape((-1,) + (1,) * (len(dims) - position - 1))

    loudness = one(*cuts[0])
    for cut in cuts[1:]:
        loudness = loudness * one(*cut)
    return loudness


def length_profile(amount, total, bound, skew):
    loads = [(1 << 20) // math.isqrt(grade ** skew) + 1 for grade in range(2, amount + 1)]
    surplus, holding = total - bound - (amount - 1), [1] * (amount - 1)
    while surplus > 0:
        movable = [i for i in range(amount - 1) if holding[i] < bound]
        pool, budget = sum([loads[i] for i in movable]), surplus
        for i in movable:
            extra = min(bound - holding[i], max(1, budget * loads[i] // pool), surplus)
            holding[i] = holding[i] + extra
            surplus = surplus - extra
    return np.array([bound] + holding)


def uneven_parts(rng, count, total, reach, lean):
    if count == 2:
        one = jax.random.randint(rng, (), max(1, total - reach), min(reach, total - 1) + 1)
        return jnp.stack([one, total - one])
    sizes = jnp.asarray(length_profile(count, total, reach, lean), jnp.int32)
    couples = (count - 1) // 2
    donor, taker = sizes[1:1 + 2 * couples:2], sizes[2:2 + 2 * couples:2]
    slack = jnp.minimum(donor - 1, reach - taker)
    shifted = jax.random.randint(jax.random.fold_in(rng, 1), (couples,), 0, 1 << 20) % (slack + 1)
    sizes = sizes.at[1:1 + 2 * couples:2].set(donor - shifted).at[2:2 + 2 * couples:2].set(taker + shifted)
    return sizes[jax.random.permutation(jax.random.fold_in(rng, 2), count)]


def bell_draw(stream_key, dims, deviation, limit, cuts=(), held_as=jnp.bfloat16):
    gain = block_levels(stream_key, dims, cuts, -0.22, 0.18) if cuts else 1.0
    array = jax.random.normal(stream_key, dims, jnp.float32) * deviation * gain
    return jnp.minimum(jnp.maximum(array, -limit), limit).astype(held_as)


def setup_inputs(seed: int = 0) -> dict:
    arg_keys = jax.random.split(jax.random.key(seed), 13)
    residual = bell_draw(arg_keys[0], (SEQ, D), 1.0, 6.0, ((0, 512),))
    out_grad = bell_draw(arg_keys[1], (SEQ, D), 1.0, 6.0, ((0, 512),))
    norm_gain = jnp.clip(1.0 + 0.15 * jax.random.normal(arg_keys[2], (D,), jnp.float32), 0.25, 1.75).astype(jnp.bfloat16)
    expert_ids = draw_expert_ids(jax.random.fold_in(arg_keys[12], 71), 0)
    route_weights = jnp.clip(0.19921875 + 0.80078125 * jax.random.uniform(arg_keys[4], (SEQ, TOPK), jnp.float32) ** block_levels(arg_keys[4], (SEQ, TOPK), ((0, 512),), -0.2, 0.2), 0.19921875, 1.0).astype(jnp.bfloat16)
    gate_up = bell_draw(arg_keys[5], (N_EXP, 2, D, FF), D ** -0.5, 0.125, ((0, 8), (2, 64)))
    down_proj = bell_draw(arg_keys[6], (N_EXP, FF, D), FF ** -0.5, 0.21875, ((0, 8), (1, 64)))
    out_proj = bell_draw(arg_keys[7], (HEADS * VD, D), (HEADS * VD) ** -0.5, 0.1875, ((0, 8),))
    queries = draw_queries(jax.random.fold_in(arg_keys[12], 71), 0)
    keys_in = draw_keys_in(jax.random.fold_in(arg_keys[12], 71), 0)
    values_in = bell_draw(arg_keys[10], (SEQ, HEADS * VD), 1.0, 6.0, ((0, 64), (1, 8)))
    segments = jnp.searchsorted(jnp.cumsum(uneven_parts(arg_keys[11], 4 * N_CTX, SEQ, REACH, 2)), jnp.arange(SEQ), side="right").astype(jnp.int32)
    return dict(residual=residual, out_grad=out_grad, norm_gain=norm_gain, expert_ids=expert_ids, route_weights=route_weights, gate_up=gate_up, down_proj=down_proj, out_proj=out_proj, queries=queries, keys_in=keys_in, values_in=values_in, segments=segments)


EPSILON = 1e-06
MASKED = -1e+30

def rounded(values):
    return lax.optimization_barrier(values.astype(jnp.bfloat16)).astype(jnp.float32)

def route_table(expert_ids, route_weights, first, count, capacity):
    tokens = expert_ids.shape[0]
    wanted = first + jnp.arange(count, dtype=jnp.int32)
    onehot = (expert_ids[:, :, None] == wanted[None, None, :]).astype(jnp.int32)
    onehot = onehot.reshape(tokens * TOPK, count)
    before = jnp.cumsum(onehot, axis=0) - onehot
    target = lax.optimization_barrier(jnp.sum(onehot * (jnp.arange(count, dtype=jnp.int32)[None, :] * capacity + before), axis=1))
    target = jnp.where(lax.optimization_barrier(jnp.sum(onehot, axis=1)) > 0, target, -1)
    slots = jnp.arange(count * capacity, dtype=jnp.int32)
    table = (target[None, :] == slots[:, None]).astype(jnp.float32)
    slot_gate = lax.optimization_barrier(jnp.sum(table * route_weights.astype(jnp.float32).reshape(1, tokens * TOPK), axis=1))
    token_table = lax.optimization_barrier(jnp.sum(table.reshape(count * capacity, tokens, TOPK), axis=2))
    return (token_table.astype(jnp.bfloat16), slot_gate.astype(jnp.bfloat16))

def swiglu_back(gate_pre, up_pre, hidden_grad):
    sigm = jax.nn.sigmoid(gate_pre)
    gate_grad = rounded(hidden_grad * up_pre * sigm * (1.0 + gate_pre * (1.0 - sigm)))
    up_grad = rounded(hidden_grad * gate_pre * sigm)
    return (gate_grad, up_grad)

def moe_grads(residual, out_grad, norm_gain, expert_ids, route_weights, gate_up, down_proj):
    gate_up_f = gate_up.astype(jnp.float32)
    down_f = down_proj.astype(jnp.float32)
    gain_f = norm_gain.astype(jnp.float32)
    blocks = SEQ // TOK_DEV

    def one_block(pieces):
        rows_in, grad_rows, id_rows, weight_rows = pieces
        feats = rows_in.astype(jnp.float32)
        inverse = lax.rsqrt(lax.optimization_barrier(jnp.mean(feats * feats, axis=1, keepdims=True)) + EPSILON)
        normed = (feats * inverse * gain_f).astype(jnp.bfloat16)
        table, slot_gate = route_table(id_rows, weight_rows, 0, N_EXP, CAP)
        slot_in = rounded(jnp.dot(table, normed, preferred_element_type=jnp.float32)).reshape(N_EXP, CAP, D)
        slot_dy = rounded(jnp.dot(table, grad_rows, preferred_element_type=jnp.float32)).reshape(N_EXP, CAP, D)
        gate_pre = jnp.einsum('ecd,edf->ecf', slot_in, gate_up_f[:, 0])
        up_pre = jnp.einsum('ecd,edf->ecf', slot_in, gate_up_f[:, 1])
        hidden_grad = slot_gate.astype(jnp.float32).reshape(N_EXP, CAP, 1) * jnp.einsum('ecd,efd->ecf', slot_dy, down_f)
        gate_grad, up_grad = swiglu_back(gate_pre, up_pre, hidden_grad)
        slot_out = jnp.einsum('ecf,edf->ecd', gate_grad, gate_up_f[:, 0]) + jnp.einsum('ecf,edf->ecd', up_grad, gate_up_f[:, 1])
        slot_out = slot_out.astype(jnp.bfloat16).reshape(N_EXP * CAP, D)
        normed_grad = lax.dot_general(table, slot_out, (((0,), (0,)), ((), ())), preferred_element_type=jnp.float32)
        scaled = normed_grad * gain_f
        cube = inverse * inverse * inverse
        total = grad_rows.astype(jnp.float32) + inverse * scaled - feats * cube * lax.optimization_barrier(jnp.mean(scaled * feats, axis=1, keepdims=True))
        return total.astype(jnp.bfloat16)
    result = lax.map(one_block, (residual.reshape(blocks, TOK_DEV, D), out_grad.reshape(blocks, TOK_DEV, D), expert_ids.reshape(blocks, TOK_DEV, TOPK), route_weights.reshape(blocks, TOK_DEV, TOPK)))
    return result.reshape(SEQ, D)

def attention_grads(queries, keys_in, values_in, head_grad, segments):
    pad = REACH
    width = pad + TOK_CTX
    key_pad = jnp.pad(keys_in, ((pad, 0), (0, 0)))
    value_pad = jnp.pad(values_in, ((pad, 0), (0, 0)))
    seg_pad = jnp.pad(segments, (pad, 0), constant_values=-1)
    scale = QK ** (-0.5)

    def one(carry, block):
        key_acc, value_acc = carry
        start = (block * TOK_CTX).astype(jnp.int32)
        query_heads = lax.dynamic_slice_in_dim(queries, start, TOK_CTX, 0).astype(jnp.float32).reshape(TOK_CTX, HEADS, QK)
        key_win = lax.dynamic_slice_in_dim(key_pad, start, width, 0).astype(jnp.float32).reshape(width, HEADS, QK)
        value_win = lax.dynamic_slice_in_dim(value_pad, start, width, 0).astype(jnp.float32).reshape(width, HEADS, VD)
        grad_heads = lax.dynamic_slice_in_dim(head_grad, start, TOK_CTX, 0).astype(jnp.float32).reshape(TOK_CTX, HEADS, VD)
        query_seg = lax.dynamic_slice_in_dim(segments, start, TOK_CTX, 0)
        key_seg = lax.dynamic_slice_in_dim(seg_pad, start, width, 0)
        query_pos = start + jnp.arange(TOK_CTX, dtype=jnp.int32)
        key_pos = start - pad + jnp.arange(width, dtype=jnp.int32)
        allowed = (query_seg[:, None] == key_seg[None, :]) & (key_pos[None, :] <= query_pos[:, None])
        scores = jnp.einsum('qhd,khd->hqk', query_heads, key_win) * scale
        scores = jnp.where(allowed[None], scores, MASKED)
        top = lax.optimization_barrier(jnp.max(scores, axis=2, keepdims=True))
        lse = top + jnp.log(lax.optimization_barrier(jnp.sum(jnp.exp(scores - top), axis=2, keepdims=True)))
        probs = jnp.exp(scores - lse)
        probs_low = rounded(probs)
        attended = rounded(jnp.einsum('hqk,khd->qhd', probs_low, value_win))
        delta = lax.optimization_barrier(jnp.sum(grad_heads * attended, axis=2))
        value_part = jnp.einsum('hqk,qhd->khd', probs_low, grad_heads).reshape(width, HEADS * VD)
        prob_grad = jnp.einsum('qhd,khd->hqk', grad_heads, value_win)
        score_grad = rounded(probs * (prob_grad - jnp.transpose(delta)[:, :, None]))
        query_part = jnp.einsum('hqk,khd->qhd', score_grad, key_win) * scale
        key_part = (jnp.einsum('hqk,qhd->khd', score_grad, query_heads) * scale).reshape(width, HEADS * QK)
        key_part = jnp.concatenate([rounded(key_part[:pad]), key_part[pad:]], axis=0)
        value_part = jnp.concatenate([rounded(value_part[:pad]), value_part[pad:]], axis=0)
        key_acc = lax.dynamic_update_slice_in_dim(key_acc, lax.dynamic_slice_in_dim(key_acc, start, width, 0) + key_part, start, 0)
        value_acc = lax.dynamic_update_slice_in_dim(value_acc, lax.dynamic_slice_in_dim(value_acc, start, width, 0) + value_part, start, 0)
        return ((key_acc, value_acc), query_part.reshape(TOK_CTX, HEADS * QK).astype(jnp.bfloat16))
    start_state = (jnp.zeros((SEQ + pad, HEADS * QK), jnp.float32), jnp.zeros((SEQ + pad, HEADS * VD), jnp.float32))
    (key_acc, value_acc), query_blocks = lax.scan(one, start_state, jnp.arange(SEQ // TOK_CTX, dtype=jnp.int32))
    query_grad = query_blocks.reshape(SEQ, HEADS * QK)
    return (query_grad, key_acc[pad:].astype(jnp.bfloat16), value_acc[pad:].astype(jnp.bfloat16))

def reference(residual, out_grad, norm_gain, expert_ids, route_weights, gate_up, down_proj, out_proj, queries, keys_in, values_in, segments):
    residual_grad = moe_grads(residual, out_grad, norm_gain, expert_ids, route_weights, gate_up, down_proj)
    head_grad = lax.dot_general(residual_grad, out_proj, (((1,), (1,)), ((), ())), preferred_element_type=jnp.float32).astype(jnp.bfloat16)
    query_grad, key_grad, value_grad = attention_grads(queries, keys_in, values_in, head_grad, segments)
    return (residual_grad, query_grad, key_grad, value_grad)
```

```python
import functools

import jax
import jax.numpy as jnp
from jax import lax
from jax.experimental import pallas as pl
from jax.experimental.pallas import tpu as pltpu
from jax.sharding import PartitionSpec as P

D = 2048
QK = 192
VD = 128
FF = 768
TOPK = 6
N_EXP = 8
N_CTX = 64
NH = 4
NY = 8
TOK = 1024
REACH = 512
TOK_DEV = 128
CAP = 24
SLOTS = 48
SHARD = 96
QB = 256
WIN = QB + REACH
N_QB = TOK // QB
EPSILON = 1e-06
MASKED = -1e30
SCALE = QK ** (-0.5)
BF = jnp.bfloat16
F32 = jnp.float32
MESH = pl.DeviceIdType.MESH


def dot_nn(a, b):
    return lax.dot_general(a, b, (((1,), (0,)), ((), ())), preferred_element_type=F32)


def dot_nt(a, b):
    return lax.dot_general(a, b, (((1,), (1,)), ((), ())), preferred_element_type=F32)


def dot_tn(a, b):
    return lax.dot_general(a, b, (((0,), (0,)), ((), ())), preferred_element_type=F32)


def scratch():
    vm, dma = pltpu.VMEM, pltpu.SemaphoreType.DMA
    return dict(
        w=vm((N_CTX, SHARD, FF), BF),
        opf=vm((N_EXP, VD, D), BF),
        lhs=vm((2 * TOK_DEV, D), BF),
        xs=vm((N_EXP, SLOTS, D), BF),
        xr=vm((N_EXP, SLOTS, D), BF),
        sel=vm((NH, 2, 256, FF), BF),
        pre=vm((256, 2 * FF), F32),
        hid=vm((256, FF), F32),
        gg=vm((192, 2 * FF), BF),
        os=vm((2, N_EXP, SLOTS, 512), BF),
        orr=vm((2, N_EXP, SLOTS, 512), BF),
        tin=vm((TOK_DEV, N_EXP * SLOTS), BF),
        tdy=vm((TOK_DEV, N_EXP * SLOTS), BF),
        inv=vm((TOK_DEV, 1), F32),
        ng=vm((TOK_DEV, D), F32),
        hs=vm((N_EXP, TOK_DEV, VD), BF),
        hr=vm((N_EXP, TOK_DEV, VD), BF),
        kw=vm((REACH + TOK, QK), BF),
        vw=vm((REACH + TOK, VD), BF),
        segh=vm((8, 128), jnp.int32),
        probs=vm((N_QB, QB, WIN), F32),
        plt=vm((N_QB, WIN, QB), BF),
        att=vm((TOK, VD), F32),
        dk=vm((REACH + TOK, QK), F32),
        dv=vm((REACH + TOK, VD), F32),
        ks=vm((REACH, QK), BF),
        vs=vm((REACH, VD), BF),
        kr=vm((REACH, QK), BF),
        vr=vm((REACH, VD), BF),
        s_local=dma((8,)),
        s_wsend=dma,
        s_w=dma((NH * NY,)),
        s_cross=dma((NH,)),
        s_halo_s=dma((3,)),
        s_halo_r=dma((3,)),
        s_op_s=dma,
        s_op_r=dma((4,)),
        s_x=dma((2,)),
        s_o=dma((4,)),
        s_h=dma((2,)),
        s_k=dma((4,)),
    )


NAMES = tuple(scratch())


def body(
    w_in, op_in, keys_in, values_in, res, dy, gain, ids, rw, seg, q,
    out_res, out_q, out_k, out_v, *rest,
):
    s = dict(zip(NAMES, rest))
    ctx, me = lax.axis_index("ctx"), lax.axis_index("exp")
    h, y, c = ctx // 16, (ctx // 2) % NY, ctx % 2
    x, l = me // 2, me % 2

    def at(hh, yy):
        return (hh * NY + yy) * 2 + c

    sibling = (ctx + 1 - 2 * c, me)
    up = (at(h, (y + 1) % NY), me)
    down = (at(h, (y + NY - 1) % NY), me)
    zs = [(at((h + k) % NH, y), me) for k in range(1, NH)]
    after = ((ctx + 1) % N_CTX, me)
    before = ((ctx + N_CTX - 1) % N_CTX, me)
    exps = [(ctx, (me + k) % N_EXP) for k in range(1, N_EXP)]
    lmate = (ctx, 2 * x + 1 - l)
    xmates = [(ctx, 2 * ((x + k) % 4) + l) for k in (2, 1, 3)]

    def send(src, dst, ssem, rsem, dev):
        pltpu.make_async_remote_copy(
            src_ref=src, dst_ref=dst, send_sem=ssem, recv_sem=rsem,
            device_id=dev, device_id_type=MESH,
        ).start()

    def wait(ref, sem):
        pltpu.make_async_copy(ref, ref, sem).wait()

    partners = [sibling, up, down, after, before] + zs + exps
    barrier = pltpu.get_barrier_semaphore()
    for dev in partners:
        pl.semaphore_signal(barrier, inc=1, device_id=dev, device_id_type=MESH)
    local = [
        pltpu.make_async_copy(w_in, s["w"].at[ctx], s["s_local"].at[0]),
        pltpu.make_async_copy(op_in, s["opf"].at[me], s["s_local"].at[1]),
        pltpu.make_async_copy(keys_in, s["kw"].at[pl.ds(REACH, TOK)], s["s_local"].at[2]),
        pltpu.make_async_copy(values_in, s["vw"].at[pl.ds(REACH, TOK)], s["s_local"].at[3]),
    ]
    for copy in local:
        copy.start()
    pl.semaphore_wait(barrier, len(partners))

    def wsend(src, hh, yy, dev):
        j = at(hh, yy)
        send(src, s["w"].at[j], s["s_wsend"], s["s_w"].at[hh * NY + yy], dev)

    def cross(src, hh, yy):
        send(src, s["w"].at[at(hh, yy)], s["s_wsend"], s["s_cross"].at[hh], sibling)

    wsend(w_in, h, y, up)
    wsend(w_in, h, y, down)
    for dev in zs:
        wsend(w_in, h, y, dev)
    cross(w_in, h, y)
    half = pl.ds(64 * c, 64)
    send(op_in.at[half], s["opf"].at[me, half], s["s_op_s"], s["s_op_r"].at[0], lmate)
    send(keys_in.at[pl.ds(REACH, REACH)], s["kw"].at[pl.ds(0, REACH)],
         s["s_halo_s"].at[0], s["s_halo_r"].at[0], after)
    send(values_in.at[pl.ds(REACH, REACH)], s["vw"].at[pl.ds(0, REACH)],
         s["s_halo_s"].at[1], s["s_halo_r"].at[1], after)
    send(seg, s["segh"], s["s_halo_s"].at[2], s["s_halo_r"].at[2], after)

    gain_f = gain[...].astype(F32)
    for r in range(0, TOK_DEV, 16):
        rows = pl.ds(r, 16)
        feats = res[rows, :].astype(F32)
        inverse = lax.rsqrt(jnp.mean(feats * feats, axis=1, keepdims=True) + EPSILON)
        s["inv"][rows, :] = inverse
        s["lhs"][rows, :] = (feats * inverse * gain_f).astype(BF)
    s["lhs"][pl.ds(TOK_DEV, TOK_DEV), :] = dy[...]

    ids_v = ids[...]
    live = ids_v < N_EXP
    expert = jnp.sum(jnp.where(live, ids_v, 0), axis=1, keepdims=True)
    weight = jnp.sum(jnp.where(live, rw[...].astype(F32), 0.0), axis=1, keepdims=True)
    lane = lax.broadcasted_iota(jnp.int32, (TOK_DEV, 128), 1)
    row = lax.broadcasted_iota(jnp.int32, (TOK_DEV, 128), 0)
    onehot = jnp.where(lane == expert, 1.0, 0.0)
    earlier = jnp.where(lane < row, 1.0, 0.0).astype(BF)
    counts = dot_nn(earlier, onehot.astype(BF))
    rank = jnp.sum(onehot * counts, axis=1, keepdims=True).astype(jnp.int32)
    place_in = expert * SLOTS + jnp.where(rank < 16, rank, rank + 16)
    place_dy = expert * SLOTS + jnp.where(rank < 16, rank + 16, rank + 24)
    slot = lax.broadcasted_iota(jnp.int32, (TOK_DEV, N_EXP * SLOTS), 1)
    hit_in = slot == place_in
    hit_dy = slot == place_dy
    s["tin"][...] = jnp.where(hit_in, weight, 0.0).astype(BF)
    s["tdy"][...] = jnp.where(hit_dy, weight, 0.0).astype(BF)
    table = jnp.concatenate(
        [jnp.where(hit_in, 1.0, 0.0).astype(BF), jnp.where(hit_dy, 1.0, 0.0).astype(BF)], axis=0
    )
    for col in range(0, D, 512):
        picked = dot_tn(table, s["lhs"][:, col : col + 512])
        s["xs"][:, :, col : col + 512] = picked.astype(BF).reshape(N_EXP, SLOTS, 512)
    for dev in exps:
        send(s["xs"].at[dev[1]], s["xr"].at[me], s["s_x"].at[0], s["s_x"].at[1], dev)
    own_x = pltpu.make_async_copy(s["xs"].at[me], s["xr"].at[me], s["s_local"].at[4])
    own_x.start()
    for dev in xmates:
        send(op_in.at[half], s["opf"].at[me, half], s["s_op_s"], s["s_op_r"].at[1], dev)

    def selection(k):
        hh = (h + k) % NH
        i = lax.broadcasted_iota(jnp.int32, (256, FF), 0)
        f = lax.broadcasted_iota(jnp.int32, (256, FF), 1)
        m = i % 16
        base = 192 * hh + 12 * (i // 16)
        first = base + jnp.where(m < 12, m, 3 * (m - 12))
        second = base + jnp.where(m >= 12, 3 * (m - 12) + 1, jnp.where(m >= 8, 3 * (m - 8) + 2, -9999))
        s["sel"][k, 0] = jnp.where(f == first, 1.0, 0.0).astype(BF)
        s["sel"][k, 1] = jnp.where(f == second, 1.0, 0.0).astype(BF)

    def halo_ready():
        wait(s["kw"].at[pl.ds(0, REACH)], s["s_halo_r"].at[0])
        wait(s["vw"].at[pl.ds(0, REACH)], s["s_halo_r"].at[1])
        wait(s["segh"], s["s_halo_r"].at[2])
        local[2].wait()
        local[3].wait()

    def seg_row(r):
        return s["segh"][4 + r : 5 + r, :] if r < 4 else seg[r - 4 : r - 3, :]

    def forward(b):
        seg_cols = jnp.transpose(seg[...].astype(F32)).astype(jnp.int32)
        seg_q = jnp.concatenate([seg_cols[:, 2 * b : 2 * b + 1], seg_cols[:, 2 * b + 1 : 2 * b + 2]], axis=0)
        pos_q = lax.broadcasted_iota(jnp.int32, (QB, 128), 0) + REACH
        pos_k = lax.broadcasted_iota(jnp.int32, (QB, 128), 1)
        scores = dot_nt(q[pl.ds(QB * b, QB), :], s["kw"][pl.ds(QB * b, WIN), :]) * SCALE
        pieces = []
        for t in range(WIN // 128):
            allowed = (seg_q == seg_row(2 * b + t)) & (pos_k + 128 * t <= pos_q)
            if 2 * b + t < 4:
                allowed = allowed & (ctx > 0)
            pieces.append(jnp.where(allowed, scores[:, 128 * t : 128 * t + 128], MASKED))
        scores = jnp.concatenate(pieces, axis=1)
        top = jnp.max(scores, axis=1, keepdims=True)
        raw = jnp.exp(scores - top)
        probs = raw / jnp.sum(raw, axis=1, keepdims=True)
        low = probs.astype(BF)
        s["probs"][b] = probs
        s["plt"][b] = jnp.transpose(low)
        s["att"][pl.ds(QB * b, QB), :] = (
            dot_nn(low, s["vw"][pl.ds(QB * b, WIN), :]).astype(BF).astype(F32)
        )

    def op_pass():
        wait(s["opf"].at[0, pl.ds(0, 64)], s["s_op_r"].at[0])
        other = lmate[1]
        for dev in xmates:
            send(s["opf"].at[other, half], s["opf"].at[other, half], s["s_op_s"], s["s_op_r"].at[2], dev)
        send(s["opf"].at[other, half], s["opf"].at[other, half], s["s_op_s"], s["s_op_r"].at[3], sibling)

    def op_cross(k, parity):
        wait(s["opf"].at[pl.ds(0, 3), pl.ds(0, 64)], s["s_op_r"].at[k])
        for step in (1, 2, 3):
            e = 2 * ((x + step) % 4) + parity
            send(s["opf"].at[e, half], s["opf"].at[e, half], s["s_op_s"], s["s_op_r"].at[3], sibling)

    def arrive(d, k):
        hh = (h + k) % NH
        if d == 0:
            if k > 0:
                wait(s["w"].at[0], s["s_w"].at[hh * NY + y])
                src = s["w"].at[at(hh, y)]
                wsend(src, hh, y, up)
                wsend(src, hh, y, down)
                cross(src, hh, y)
            return
        ways = [(1, (y + NY - d) % NY, up), (-1, (y + d) % NY, down)]
        if d == 4:
            ways = ways[:1]
        for way, yy, dev in ways:
            wait(s["w"].at[0], s["s_w"].at[hh * NY + yy])
            src = s["w"].at[at(hh, yy)]
            if d < 3 or (d == 3 and (k < 2) == (way == 1)):
                wsend(src, hh, yy, dev)
            cross(src, hh, yy)

    def experts(k):
        hh = (h + k) % NH
        wait(s["w"].at[pl.ds(0, NY)], s["s_cross"].at[hh])
        block = pl.ds(16 * hh, 16)
        cols = pl.ds(pl.multiple_of(512 * hh, 512), 512)
        xr, w = s["xr"], s["w"]

        def stacked(first, columns):
            lead = xr[:, first : first + 16, columns].reshape(128, -1)
            tail = xr[:, 32:48, columns].reshape(128, -1)
            return jnp.concatenate([lead, tail], axis=0)

        rows_in = stacked(0, cols)
        gate = dot_nn(rows_in, w[block, 0:32, :].reshape(512, FF))
        upper = dot_nn(rows_in, w[block, 32:64, :].reshape(512, FF))
        if k == 0:
            s["pre"][:, 0:FF] = gate
            s["pre"][:, FF : 2 * FF] = upper
        else:
            s["pre"][:, 0:FF] += gate
            s["pre"][:, FF : 2 * FF] += upper
        d0 = w[block, 64:80, :].reshape(256, FF)
        d1 = w[block, 80:96, :].reshape(256, FF)
        h0 = dot_nt(stacked(16, slice(0, 768)), d0) + dot_nt(stacked(16, slice(768, 1536)), d1)
        last = stacked(16, slice(1536, 2048))
        h1 = dot_nt(last, d0[:, 0:512])
        h2 = dot_nt(last[:, 0:256], d0[:, 512:768]) + dot_nt(last[:, 256:512], d1[:, 0:256])
        h3 = dot_nt(last, d1[:, 256:768])
        m = lax.broadcasted_iota(jnp.int32, (256, 256), 1) % 16
        z1 = jnp.where(m < 12, h0, h1)
        z2 = jnp.where(m < 12, pltpu.roll(h3, 252, 1), h2)
        hid = dot_nn(z1.astype(BF), s["sel"][k, 0]) + dot_nn(z2.astype(BF), s["sel"][k, 1])
        if k == 0:
            s["hid"][...] = hid
        else:
            s["hid"][...] += hid

    work = [
        [lambda: selection(0), lambda: selection(1)],
        [lambda: selection(2), lambda: selection(3)],
        [op_pass, halo_ready, lambda: forward(0)],
        [lambda: forward(1)],
        [lambda: op_cross(1, l), lambda: forward(2)],
        [lambda: forward(3)],
        [lambda: op_cross(2, 1 - l)],
    ]
    for d in range(0, 4):
        for k in range(NH):
            arrive(d, k)
            if d > 0 and work:
                for piece in work.pop(0):
                    piece()
    local[0].wait()
    own_x.wait()
    wait(s["xr"].at[pl.ds(0, 7)], s["s_x"].at[1])
    for k in range(NH):
        arrive(4, k)
    for k in range(NH):
        experts(k)

    for part in range(6):
        if part < 4:
            rows = slice(32 * part, 32 * part + 32)
            gate = s["pre"][rows, 0:FF]
            upper = s["pre"][rows, FF : 2 * FF]
            hid = s["hid"][rows, :]
        else:
            rows = slice(128 + 64 * (part - 4), 192 + 64 * (part - 4))
            gate = s["pre"][rows, 0:FF].reshape(4, 16, FF)[:, 0:8].reshape(32, FF)
            upper = s["pre"][rows, FF : 2 * FF].reshape(4, 16, FF)[:, 0:8].reshape(32, FF)
            hid = s["hid"][rows, :].reshape(4, 16, FF)[:, 8:16].reshape(32, FF)
        sigm = jax.nn.sigmoid(gate)
        put = pl.ds(32 * part, 32)
        s["gg"][put, 0:FF] = (hid * upper * sigm * (1.0 + gate * (1.0 - sigm))).astype(BF)
        s["gg"][put, FF : 2 * FF] = (hid * gate * sigm).astype(BF)

    gg, os = s["gg"], s["os"]

    def slot_grad(n):
        block = pl.ds(8 * n, 8)
        return dot_nt(gg[:, 0:FF], s["w"][block, 0:32, :].reshape(256, FF)) + dot_nt(
            gg[:, FF : 2 * FF], s["w"][block, 32:64, :].reshape(256, FF)
        )

    own_o = []
    for buf in range(2):
        for sub in range(2):
            cols = pl.ds(256 * sub, 256)
            o0 = slot_grad(4 * buf + sub)
            o1 = slot_grad(4 * buf + 2 + sub)
            os[buf, :, 0:16, cols] = o0[0:128].astype(BF).reshape(N_EXP, 16, 256)
            os[buf, :, 16:32, cols] = o1[0:128].astype(BF).reshape(N_EXP, 16, 256)
            tail = jnp.concatenate(
                [o0[128:192].reshape(N_EXP, 8, 256), o1[128:192].reshape(N_EXP, 8, 256)], axis=1
            )
            os[buf, :, 32:48, cols] = tail.astype(BF)
        for dev in exps:
            send(os.at[buf, dev[1]], s["orr"].at[buf, me], s["s_o"].at[buf], s["s_o"].at[2 + buf], dev)
        copy = pltpu.make_async_copy(os.at[buf, me], s["orr"].at[buf, me], s["s_local"].at[5 + buf])
        copy.start()
        own_o.append(copy)

    for buf in range(2):
        own_o[buf].wait()
        wait(s["orr"].at[buf, pl.ds(0, 7)], s["s_o"].at[2 + buf])
        got = s["orr"][buf].reshape(N_EXP * SLOTS, 512)
        s["ng"][:, 1024 * buf : 1024 * buf + 512] = dot_nn(s["tin"][...], got)
        s["ng"][:, 1024 * buf + 512 : 1024 * buf + 1024] = dot_nn(s["tdy"][...], got)
    for r in range(0, TOK_DEV, 16):
        rows = pl.ds(r, 16)
        inverse = s["inv"][rows, :]
        scaled = s["ng"][rows, :] * gain_f
        feats = res[rows, :].astype(F32)
        mean = jnp.mean(scaled * feats, axis=1, keepdims=True)
        total = dy[rows, :].astype(F32) + inverse * scaled - feats * (inverse * inverse * inverse * mean)
        out_res[rows, :] = total.astype(BF)

    local[1].wait()
    wait(s["opf"].at[pl.ds(0, 7), pl.ds(0, 64)], s["s_op_r"].at[3])
    own_h = None
    for step in (2, 1, 3, 0):
        pair = (x + step) % 4
        proj = s["opf"][pl.ds(2 * pair, 2)].reshape(2 * VD, D)
        grads = dot_nt(out_res[...], proj).astype(BF)
        s["hs"][2 * pair] = grads[:, 0:VD]
        s["hs"][2 * pair + 1] = grads[:, VD : 2 * VD]
        for parity in (0, 1):
            if step:
                e = 2 * pair + parity
                send(s["hs"].at[e], s["hr"].at[me], s["s_h"].at[0], s["s_h"].at[1], (ctx, e))
        if not step:
            e = lmate[1]
            send(s["hs"].at[e], s["hr"].at[me], s["s_h"].at[0], s["s_h"].at[1], (ctx, e))
            own_h = pltpu.make_async_copy(s["hs"].at[me], s["hr"].at[me], s["s_local"].at[7])
            own_h.start()
    s["dk"][...] = jnp.zeros((REACH + TOK, QK), F32)
    s["dv"][...] = jnp.zeros((REACH + TOK, VD), F32)
    own_h.wait()
    wait(s["hr"].at[pl.ds(0, 7)], s["s_h"].at[1])

    for b in range(N_QB):
        rows, window = pl.ds(QB * b, QB), pl.ds(QB * b, WIN)
        grad = s["hr"][2 * b : 2 * b + 2].reshape(QB, VD)
        delta = jnp.sum(grad.astype(F32) * s["att"][rows, :], axis=1, keepdims=True)
        prob_grad = dot_nt(grad, s["vw"][window, :])
        score_grad = (s["probs"][b] * (prob_grad - delta)).astype(BF)
        s["dv"][window, :] += dot_nn(s["plt"][b], grad)
        s["dk"][window, :] += dot_tn(score_grad, q[rows, :])
        out_q[rows, :] = (dot_nn(score_grad, s["kw"][window, :]) * SCALE).astype(BF)
        if b == 1:
            s["ks"][...] = (s["dk"][0:REACH, :] * SCALE).astype(BF)
            s["vs"][...] = s["dv"][0:REACH, :].astype(BF)
            send(s["ks"], s["kr"], s["s_k"].at[0], s["s_k"].at[1], before)
            send(s["vs"], s["vr"], s["s_k"].at[2], s["s_k"].at[3], before)
    out_k[0:REACH, :] = (s["dk"][REACH : 2 * REACH, :] * SCALE).astype(BF)
    out_v[0:REACH, :] = s["dv"][REACH : 2 * REACH, :].astype(BF)
    wait(s["kr"], s["s_k"].at[1])
    out_k[REACH:TOK, :] = (
        s["dk"][2 * REACH : 3 * REACH, :] * SCALE + s["kr"][...].astype(F32)
    ).astype(BF)
    wait(s["vr"], s["s_k"].at[3])
    out_v[REACH:TOK, :] = (s["dv"][2 * REACH : 3 * REACH, :] + s["vr"][...].astype(F32)).astype(BF)

    wait(s["w"].at[pl.ds(0, 63)], s["s_wsend"])
    wait(s["opf"].at[pl.ds(0, 7)], s["s_op_s"])
    wait(keys_in.at[pl.ds(0, REACH)], s["s_halo_s"].at[0])
    wait(values_in.at[pl.ds(0, REACH)], s["s_halo_s"].at[1])
    wait(s["segh"], s["s_halo_s"].at[2])
    wait(s["xs"].at[pl.ds(0, 7)], s["s_x"].at[0])
    for buf in range(2):
        wait(os.at[buf, pl.ds(0, 7)], s["s_o"].at[buf])
    wait(s["hs"].at[pl.ds(0, 7)], s["s_h"].at[0])
    wait(s["ks"], s["s_k"].at[0])
    wait(s["vs"], s["s_k"].at[2])


def shards(
    residual, out_grad, norm_gain, expert_ids, route_weights, gate_up, down_proj, out_proj,
    queries, keys_in, values_in, segments,
):
    down = down_proj.reshape(12, D)
    packed = jnp.concatenate([down[:, :1536], down[:, 1536:].reshape(4, 1536)], axis=0)
    share = jnp.concatenate([gate_up.reshape(64, FF), packed[:, :FF], packed[:, FF:]], axis=0)
    vm = pl.BlockSpec(memory_space=pltpu.VMEM)
    hbm = pl.BlockSpec(memory_space=pl.ANY)
    return pl.pallas_call(
        body,
        out_shape=(
            jax.ShapeDtypeStruct((TOK_DEV, D), BF),
            jax.ShapeDtypeStruct((TOK, QK), BF),
            jax.ShapeDtypeStruct((TOK, QK), BF),
            jax.ShapeDtypeStruct((TOK, VD), BF),
        ),
        in_specs=[hbm] * 4 + [vm] * 7,
        out_specs=(vm,) * 4,
        scratch_shapes=list(scratch().values()),
        compiler_params=pltpu.CompilerParams(
            collective_id=0, has_side_effects=True, vmem_limit_bytes=60 * 1024 * 1024
        ),
    )(
        share, out_proj, keys_in, values_in, residual, out_grad, norm_gain.reshape(1, D),
        expert_ids, route_weights, segments.reshape(8, 128), queries,
    )


def solution(mesh):
    return jax.shard_map(
        shards,
        mesh=mesh,
        in_specs=(
            P(("ctx", "exp"), None),
            P(("ctx", "exp"), None),
            P(),
            P(("ctx", "exp"), None),
            P(("ctx", "exp"), None),
            P("exp", None, "ctx", None),
            P("exp", "ctx", None),
            P("exp", None),
            P("ctx", "exp"),
            P("ctx", "exp"),
            P("ctx", "exp"),
            P("ctx"),
        ),
        out_specs=(P(("ctx", "exp"), None), P("ctx", "exp"), P("ctx", "exp"), P("ctx", "exp")),
        check_vma=False,
    )
```

```python
import functools

import jax
import jax.numpy as jnp
from jax import lax
from jax.experimental import pallas as pl
from jax.experimental.pallas import tpu as pltpu
from jax.sharding import PartitionSpec as P

D = 2048
QK = 192
VD = 128
FF = 768
TOPK = 6
N_EXP = 8
N_CTX = 64
NH = 4
NY = 8
TOK = 1024
REACH = 512
TOK_DEV = 128
CAP = 24
SLOTS = 48
LIVE = N_EXP * CAP
SHARD = 96
QB = 256
WIN = QB + REACH
N_QB = TOK // QB
EPSILON = 1e-06
MASKED = -1e30
SCALE = QK ** (-0.5)
BF = jnp.bfloat16
F32 = jnp.float32
MESH = pl.DeviceIdType.MESH


def dot_nn(a, b):
    return lax.dot_general(a, b, (((1,), (0,)), ((), ())), preferred_element_type=F32)


def dot_nt(a, b):
    return lax.dot_general(a, b, (((1,), (1,)), ((), ())), preferred_element_type=F32)


def dot_tn(a, b):
    return lax.dot_general(a, b, (((0,), (0,)), ((), ())), preferred_element_type=F32)


def scratch():
    vm, dma = pltpu.VMEM, pltpu.SemaphoreType.DMA
    return dict(
        w=vm((N_CTX, SHARD, FF), BF),
        opf=vm((N_EXP, VD, D), BF),
        lhs=vm((2 * TOK_DEV, D), BF),
        xs=vm((N_EXP, SLOTS, D), BF),
        xr=vm((N_EXP, SLOTS, D), BF),
        sel=vm((NH, 2, 256, FF), BF),
        pre=vm((256, 2 * FF), F32),
        hid=vm((256, FF), F32),
        gg=vm((LIVE, 2 * FF), BF),
        os=vm((2, N_EXP, SLOTS, 512), BF),
        orr=vm((2, N_EXP, SLOTS, 512), BF),
        tin=vm((TOK_DEV, N_EXP * SLOTS), BF),
        tdy=vm((TOK_DEV, N_EXP * SLOTS), BF),
        inv=vm((TOK_DEV, 1), F32),
        auxs=vm((N_EXP, CAP, 128), F32),
        auxr=vm((N_EXP, CAP, 128), F32),
        places=vm((8, 128), jnp.int32),
        placer=vm((N_EXP, 8, 128), jnp.int32),
        tab=vm((N_EXP, TOK_DEV, 256), BF),
        ng=vm((LIVE, D), F32),
        rg=vm((LIVE, D), BF),
        hs=vm((N_EXP, LIVE, VD), BF),
        hr=vm((N_EXP, LIVE, VD), BF),
        grads=vm((TOK, VD), BF),
        kw=vm((QK, REACH + TOK), BF),
        vw=vm((REACH + TOK, VD), BF),
        segh=vm((8, 128), jnp.int32),
        probs=vm((N_QB, QB, WIN), F32),
        plt=vm((N_QB, WIN, QB), BF),
        att=vm((TOK, VD), F32),
        dk=vm((QK, REACH + TOK), F32),
        dv=vm((REACH + TOK, VD), F32),
        ks=vm((QK, REACH), BF),
        vs=vm((REACH, VD), BF),
        kr=vm((QK, REACH), BF),
        vr=vm((REACH, VD), BF),
        s_local=dma((10,)),
        s_wsend=dma,
        s_w=dma((NH * NY,)),
        s_cross=dma((NH,)),
        s_halo_s=dma((3,)),
        s_halo_r=dma((3,)),
        s_op_s=dma,
        s_op_r=dma((4,)),
        s_x=dma((2,)),
        s_aux=dma((4,)),
        s_o=dma((4,)),
        s_h=dma((2,)),
        s_k=dma((4,)),
    )


NAMES = tuple(scratch())


def body(
    gu_in, op_in, keys_in, values_in, down_in, res, dy, gain, ids, rw, seg, qt,
    out_res, out_q, out_k, out_v, *rest,
):
    s = dict(zip(NAMES, rest))
    ctx, me = lax.axis_index("ctx"), lax.axis_index("exp")
    h, y, c = ctx // 16, (ctx // 2) % NY, ctx % 2
    x, l = me // 2, me % 2

    def at(hh, yy):
        return (hh * NY + yy) * 2 + c

    sibling = (ctx + 1 - 2 * c, me)
    up = (at(h, (y + 1) % NY), me)
    down = (at(h, (y + NY - 1) % NY), me)
    zs = [(at((h + k) % NH, y), me) for k in range(1, NH)]
    after = ((ctx + 1) % N_CTX, me)
    before = ((ctx + N_CTX - 1) % N_CTX, me)
    exps = [(ctx, (me + k) % N_EXP) for k in range(1, N_EXP)]
    lmate = (ctx, 2 * x + 1 - l)
    xmates = [(ctx, 2 * ((x + k) % 4) + l) for k in (2, 1, 3)]

    def send(src, dst, ssem, rsem, dev):
        pltpu.make_async_remote_copy(
            src_ref=src, dst_ref=dst, send_sem=ssem, recv_sem=rsem,
            device_id=dev, device_id_type=MESH,
        ).start()

    def wait(ref, sem):
        pltpu.make_async_copy(ref, ref, sem).wait()

    partners = [sibling, up, down, after, before] + zs + exps
    barrier = pltpu.get_barrier_semaphore()
    for dev in partners:
        pl.semaphore_signal(barrier, inc=1, device_id=dev, device_id_type=MESH)
    local = [
        pltpu.make_async_copy(gu_in, s["w"].at[ctx, pl.ds(0, 64)], s["s_local"].at[0]),
        pltpu.make_async_copy(op_in, s["opf"].at[me], s["s_local"].at[1]),
        pltpu.make_async_copy(keys_in, s["kw"].at[:, pl.ds(REACH, TOK)], s["s_local"].at[2]),
        pltpu.make_async_copy(values_in, s["vw"].at[pl.ds(REACH, TOK)], s["s_local"].at[3]),
    ]
    for copy in local:
        copy.start()
    rows12 = down_in[...].astype(F32)
    tail = [
        jnp.concatenate([rows12[3 * a + b : 3 * a + b + 1, 1536:2048] for a in range(4)], axis=0)
        for b in range(3)
    ]
    rows16 = jnp.concatenate([rows12[:, 0:1536], jnp.concatenate(tail, axis=1)], axis=0).astype(BF)
    s["w"][ctx, 64:80, :] = rows16[:, 0:768]
    s["w"][ctx, 80:96, :] = rows16[:, 768:1536]
    local[0].wait()
    w_in = s["w"].at[ctx]
    pl.semaphore_wait(barrier, len(partners))

    def wsend(src, hh, yy, dev):
        j = at(hh, yy)
        send(src, s["w"].at[j], s["s_wsend"], s["s_w"].at[hh * NY + yy], dev)

    def cross(src, hh, yy):
        send(src, s["w"].at[at(hh, yy)], s["s_wsend"], s["s_cross"].at[hh], sibling)

    wsend(w_in, h, y, up)
    wsend(w_in, h, y, down)
    for dev in zs:
        wsend(w_in, h, y, dev)
    cross(w_in, h, y)
    half = pl.ds(64 * c, 64)
    send(op_in.at[half], s["opf"].at[me, half], s["s_op_s"], s["s_op_r"].at[0], lmate)
    for dev in xmates:
        send(op_in.at[half], s["opf"].at[me, half], s["s_op_s"], s["s_op_r"].at[1], dev)
    send(keys_in.at[:, pl.ds(REACH, REACH)], s["kw"].at[:, pl.ds(0, REACH)],
         s["s_halo_s"].at[0], s["s_halo_r"].at[0], after)
    send(values_in.at[pl.ds(REACH, REACH)], s["vw"].at[pl.ds(0, REACH)],
         s["s_halo_s"].at[1], s["s_halo_r"].at[1], after)
    send(seg, s["segh"], s["s_halo_s"].at[2], s["s_halo_r"].at[2], after)

    gain_rows = gain[...].astype(F32)
    gain_f = jnp.concatenate([gain_rows[i : i + 1, :] for i in range(16)], axis=1)

    def normalize():
        for r in range(0, TOK_DEV, 16):
            rows = pl.ds(r, 16)
            feats = res[rows, :].astype(F32)
            inverse = lax.rsqrt(jnp.mean(feats * feats, axis=1, keepdims=True) + EPSILON)
            s["inv"][rows, :] = inverse
            s["lhs"][rows, :] = (feats * inverse * gain_f).astype(BF)
        s["lhs"][pl.ds(TOK_DEV, TOK_DEV), :] = dy[...]

    ids_v = ids[...]
    live = ids_v < N_EXP
    expert = jnp.sum(jnp.where(live, ids_v, 0), axis=0, keepdims=True)
    first = lax.broadcasted_iota(jnp.int32, (TOK_DEV, TOK_DEV), 0)
    second = lax.broadcasted_iota(jnp.int32, (TOK_DEV, TOK_DEV), 1)
    earlier = jnp.where(first < second, 1.0, 0.0).astype(BF)
    onehot = jnp.where(lax.broadcasted_iota(jnp.int32, (16, TOK_DEV), 0) == expert, 1.0, 0.0)
    counts = dot_nn(onehot.astype(BF), earlier)
    rank = jnp.sum(onehot * counts, axis=0, keepdims=True).astype(jnp.int32)
    place_in = expert * SLOTS + jnp.where(rank < 16, rank, rank + 16)
    place_dy = expert * SLOTS + jnp.where(rank < 16, rank + 16, rank + 24)
    slot = lax.broadcasted_iota(jnp.int32, (N_EXP * SLOTS, TOK_DEV), 0)
    hit_in = jnp.where(slot == place_in, 1.0, 0.0).astype(BF)
    hit_dy = jnp.where(slot == place_dy, 1.0, 0.0).astype(BF)

    def dispatch(*columns):
        table = jnp.concatenate([hit_in, hit_dy], axis=1)
        for col in columns:
            picked = dot_nn(table, s["lhs"][:, col : col + 512])
            s["xs"][:, :, col : col + 512] = picked.astype(BF).reshape(N_EXP, SLOTS, 512)

    own = [
        pltpu.make_async_copy(s["xs"].at[me], s["xr"].at[me], s["s_local"].at[4]),
        pltpu.make_async_copy(s["auxs"].at[me], s["auxr"].at[me], s["s_local"].at[8]),
        pltpu.make_async_copy(s["places"], s["placer"].at[me], s["s_local"].at[9]),
    ]

    def dispatch_send():
        for dev in exps:
            send(s["xs"].at[dev[1]], s["xr"].at[me], s["s_x"].at[0], s["s_x"].at[1], dev)
        own[0].start()

    def side_send():
        weight = jnp.sum(jnp.where(live, rw[...].astype(F32), 0.0), axis=0, keepdims=True)
        weight = jnp.transpose(jnp.broadcast_to(weight, (8, TOK_DEV)))[:, 0:1]
        inverse = s["inv"][...]
        high = inverse.astype(BF).astype(F32)
        mid = (inverse - high).astype(BF).astype(F32)
        low = inverse - high - mid
        lane = lax.broadcasted_iota(jnp.int32, (TOK_DEV, 128), 1)
        terms = jnp.where(lane == 0, high, jnp.where(lane == 1, mid, jnp.where(lane == 2, low, jnp.where(lane == 3, weight, 0.0))))
        picked = dot_nn(hit_in, terms.astype(BF)).reshape(N_EXP, SLOTS, 128)
        s["auxs"][:, 0:16, :] = picked[:, 0:16]
        s["auxs"][:, 16:24, :] = picked[:, 32:40]
        code = expert * 16 + jnp.where(rank < 16, rank, rank + 112 + 8 * (me % 2))
        s["places"][...] = jnp.broadcast_to(code, (8, 128))
        for dev in exps:
            send(s["auxs"].at[dev[1]], s["auxr"].at[me], s["s_aux"].at[0], s["s_aux"].at[1], dev)
            send(s["places"], s["placer"].at[me], s["s_aux"].at[2], s["s_aux"].at[3], dev)
        own[1].start()
        own[2].start()

    def tables():
        s["tin"][...] = jnp.transpose(hit_in)
        s["tdy"][...] = jnp.transpose(hit_dy)

    def places_ready():
        own[2].wait()
        wait(s["placer"].at[pl.ds(0, 7)], s["s_aux"].at[3])

    def place_table(src):
        at_row = lax.broadcasted_iota(jnp.int32, (256, TOK_DEV), 0) == s["placer"][src, 0:1, :]
        s["tab"][src] = jnp.transpose(jnp.where(at_row, 1.0, 0.0).astype(BF))

    def rows_ready():
        own[0].wait()
        own[1].wait()
        wait(s["xr"].at[pl.ds(0, 7)], s["s_x"].at[1])
        wait(s["auxr"].at[pl.ds(0, 7)], s["s_aux"].at[1])

    def selection(k):
        hh = (h + k) % NH
        i = lax.broadcasted_iota(jnp.int32, (256, FF), 0)
        f = lax.broadcasted_iota(jnp.int32, (256, FF), 1)
        m = i % 16
        base = 192 * hh + 12 * (i // 16)
        first = base + jnp.where(m < 12, m, 3 * (m - 12))
        second = base + jnp.where(m >= 12, 3 * (m - 12) + 1, jnp.where(m >= 8, 3 * (m - 8) + 2, -9999))
        s["sel"][k, 0] = jnp.where(f == first, 1.0, 0.0).astype(BF)
        s["sel"][k, 1] = jnp.where(f == second, 1.0, 0.0).astype(BF)

    def halo_ready():
        wait(s["kw"].at[:, pl.ds(0, REACH)], s["s_halo_r"].at[0])
        wait(s["vw"].at[pl.ds(0, REACH)], s["s_halo_r"].at[1])
        wait(s["segh"], s["s_halo_r"].at[2])
        local[2].wait()
        local[3].wait()

    def seg_row(r):
        return s["segh"][4 + r : 5 + r, :] if r < 4 else seg[r - 4 : r - 3, :]

    def forward(b):
        seg_cols = jnp.transpose(seg[...].astype(F32)).astype(jnp.int32)
        seg_q = jnp.concatenate([seg_cols[:, 2 * b : 2 * b + 1], seg_cols[:, 2 * b + 1 : 2 * b + 2]], axis=0)
        pos_q = lax.broadcasted_iota(jnp.int32, (QB, 128), 0) + REACH
        pos_k = lax.broadcasted_iota(jnp.int32, (QB, 128), 1)
        scores = dot_nn(jnp.transpose(qt[:, pl.ds(QB * b, QB)]), s["kw"][:, pl.ds(QB * b, WIN)]) * SCALE
        pieces = []
        for t in range(WIN // 128):
            allowed = (seg_q == seg_row(2 * b + t)) & (pos_k + 128 * t <= pos_q)
            if 2 * b + t < 4:
                allowed = allowed & (ctx > 0)
            pieces.append(jnp.where(allowed, scores[:, 128 * t : 128 * t + 128], MASKED))
        scores = jnp.concatenate(pieces, axis=1)
        top = jnp.max(scores, axis=1, keepdims=True)
        raw = jnp.exp(scores - top)
        probs = raw / jnp.sum(raw, axis=1, keepdims=True)
        low = probs.astype(BF)
        s["probs"][b] = probs
        s["plt"][b] = jnp.transpose(low)
        s["att"][pl.ds(QB * b, QB), :] = (
            dot_nn(low, s["vw"][pl.ds(QB * b, WIN), :]).astype(BF).astype(F32)
        )

    def op_pass():
        wait(s["opf"].at[0, pl.ds(0, 64)], s["s_op_r"].at[0])
        other = lmate[1]
        for dev in xmates:
            send(s["opf"].at[other, half], s["opf"].at[other, half], s["s_op_s"], s["s_op_r"].at[2], dev)
        send(s["opf"].at[other, half], s["opf"].at[other, half], s["s_op_s"], s["s_op_r"].at[3], sibling)

    def op_cross(k, parity):
        wait(s["opf"].at[pl.ds(0, 3), pl.ds(0, 64)], s["s_op_r"].at[k])
        for step in (1, 2, 3):
            e = 2 * ((x + step) % 4) + parity
            send(s["opf"].at[e, half], s["opf"].at[e, half], s["s_op_s"], s["s_op_r"].at[3], sibling)

    def arrive(d, k, way):
        hh = (h + k) % NH
        yy = (y + NY - way * d) % NY
        if d + k > 0:
            wait(s["w"].at[0], s["s_w"].at[hh * NY + yy])
            src = s["w"].at[at(hh, yy)]
            if d == 0:
                wsend(src, hh, yy, up)
                wsend(src, hh, yy, down)
            elif d < 3 or (d == 3 and (k < 2) == (way == 1)):
                wsend(src, hh, yy, up if way == 1 else down)
            cross(src, hh, yy)

    def experts(k):
        hh = (h + k) % NH
        wait(s["w"].at[pl.ds(0, NY)], s["s_cross"].at[hh])
        block = pl.ds(16 * hh, 16)
        cols = pl.ds(pl.multiple_of(512 * hh, 512), 512)
        xr, w = s["xr"], s["w"]

        def stacked(first, columns):
            lead = xr[:, first : first + 16, columns].reshape(128, -1)
            tail = xr[:, 32:48, columns].reshape(128, -1)
            return jnp.concatenate([lead, tail], axis=0)

        rows_in = stacked(0, cols)
        gate = dot_nn(rows_in, w[block, 0:32, :].reshape(512, FF))
        upper = dot_nn(rows_in, w[block, 32:64, :].reshape(512, FF))
        if k == 0:
            s["pre"][:, 0:FF] = gate
            s["pre"][:, FF : 2 * FF] = upper
        else:
            s["pre"][:, 0:FF] += gate
            s["pre"][:, FF : 2 * FF] += upper
        d0 = w[block, 64:80, :].reshape(256, FF)
        d1 = w[block, 80:96, :].reshape(256, FF)
        h0 = dot_nt(stacked(16, slice(0, 768)), d0) + dot_nt(stacked(16, slice(768, 1536)), d1)
        last = stacked(16, slice(1536, 2048))
        h1 = dot_nt(last, d0[:, 0:512])
        h2 = dot_nt(last[:, 0:256], d0[:, 512:768]) + dot_nt(last[:, 256:512], d1[:, 0:256])
        h3 = dot_nt(last, d1[:, 256:768])
        m = lax.broadcasted_iota(jnp.int32, (256, 256), 1) % 16
        z1 = jnp.where(m < 12, h0, h1)
        z2 = jnp.where(m < 12, pltpu.roll(h3, 252, 1), h2)
        hid = dot_nn(z1.astype(BF), s["sel"][k, 0]) + dot_nn(z2.astype(BF), s["sel"][k, 1])
        if k == 0:
            s["hid"][...] = hid
        else:
            s["hid"][...] += hid

    normalize()
    steps = [
        (1, 0, -1), (1, 0, 1),
        lambda: dispatch(0, 512),
        (0, 1, 0), (0, 3, 0),
        lambda: dispatch(1024, 1536), dispatch_send,
        (2, 0, -1), (2, 0, 1),
        side_send,
        (1, 1, -1), (1, 1, 1), (0, 2, 0),
        tables, lambda: selection(0),
        (1, 3, -1), (1, 3, 1),
        lambda: selection(1), op_pass,
        (3, 0, -1), (3, 0, 1),
        halo_ready, lambda: forward(0),
        (2, 1, -1), (2, 1, 1),
        lambda: forward(1),
        (1, 2, -1), (1, 2, 1),
        lambda: forward(2), lambda: op_cross(1, l),
        (2, 3, -1), (2, 3, 1),
        lambda: forward(3),
        (3, 1, -1), (4, 0, 1),
        places_ready, lambda: [place_table(src) for src in range(4)],
        (2, 2, -1), (3, 1, 1),
        lambda: [place_table(src) for src in range(4, 8)], lambda: selection(2),
        (2, 2, 1), (3, 3, -1),
        lambda: selection(3), rows_ready, lambda: experts(0),
        (3, 2, -1), (3, 3, 1),
        lambda: op_cross(2, 1 - l),
        (4, 1, 1), (4, 3, -1),
        lambda: experts(1),
        (3, 2, 1), (4, 2, -1),
        lambda: experts(3), lambda: experts(2),
    ]
    for step in steps:
        if callable(step):
            step()
        else:
            arrive(*step)

    for part in range(6):
        if part < 4:
            rows = slice(32 * part, 32 * part + 32)
            gate = s["pre"][rows, 0:FF]
            upper = s["pre"][rows, FF : 2 * FF]
            hid = s["hid"][rows, :]
        else:
            rows = slice(128 + 64 * (part - 4), 192 + 64 * (part - 4))
            gate = s["pre"][rows, 0:FF].reshape(4, 16, FF)[:, 0:8].reshape(32, FF)
            upper = s["pre"][rows, FF : 2 * FF].reshape(4, 16, FF)[:, 0:8].reshape(32, FF)
            hid = s["hid"][rows, :].reshape(4, 16, FF)[:, 8:16].reshape(32, FF)
        sigm = jax.nn.sigmoid(gate)
        put = pl.ds(32 * part, 32)
        s["gg"][put, 0:FF] = (hid * upper * sigm * (1.0 + gate * (1.0 - sigm))).astype(BF)
        s["gg"][put, FF : 2 * FF] = (hid * gate * sigm).astype(BF)

    gg, os = s["gg"], s["os"]
    xr = s["xr"]
    side = jnp.concatenate(
        [s["auxr"][:, 0:16, :].reshape(128, 128), s["auxr"][:, 16:24, :].reshape(64, 128)], axis=0
    )
    inverse = side[:, 0:1] + side[:, 1:2] + side[:, 2:3]
    weight = side[:, 3:4]

    def slot_rows(first, cols):
        lead = xr[:, 16 * first : 16 * first + 16, cols].reshape(128, -1).astype(F32)
        tail = xr[:, 32:48, cols].astype(F32)[:, 8 * first : 8 * first + 8].reshape(64, -1)
        return jnp.concatenate([lead, tail], axis=0)

    dots = jnp.zeros((LIVE, 128), F32)
    for n in range(8):
        block, cols = pl.ds(8 * n, 8), pl.ds(256 * n, 256)
        grad = weight * (
            dot_nt(gg[:, 0:FF], s["w"][block, 0:32, :].reshape(256, FF))
            + dot_nt(gg[:, FF : 2 * FF], s["w"][block, 32:64, :].reshape(256, FF))
        )
        s["ng"][:, cols] = grad
        prod = grad * slot_rows(0, cols)
        dots = dots + prod[:, 0:128] + prod[:, 128:256]
    share = inverse * (jnp.sum(dots, axis=1, keepdims=True) / D)
    gain_inv = 1.0 / gain_f

    def total(n):
        cols = pl.ds(256 * n, 256)
        lanes = slice(256 * n, 256 * n + 256)
        value = (
            slot_rows(1, cols)
            + inverse * (s["ng"][:, cols] * gain_f[:, lanes])
            - slot_rows(0, cols) * share * gain_inv[:, lanes]
        )
        s["rg"][:, cols] = value.astype(BF)
        return value

    for buf in range(2):
        for sub in range(2):
            cols = pl.ds(256 * sub, 256)
            o0 = total(4 * buf + sub)
            o1 = total(4 * buf + 2 + sub)
            os[buf, :, 0:16, cols] = o0[0:128].astype(BF).reshape(N_EXP, 16, 256)
            os[buf, :, 16:32, cols] = o1[0:128].astype(BF).reshape(N_EXP, 16, 256)
            tail = jnp.concatenate(
                [o0[128:192].reshape(N_EXP, 8, 256), o1[128:192].reshape(N_EXP, 8, 256)], axis=1
            )
            os[buf, :, 32:48, cols] = tail.astype(BF)

    local[1].wait()
    wait(s["opf"].at[pl.ds(0, 7), pl.ds(0, 64)], s["s_op_r"].at[3])
    own_h = None
    for step in (2, 1, 3, 0):
        pair = (x + step) % 4
        proj = s["opf"][pl.ds(2 * pair, 2)].reshape(2 * VD, D)
        grads = dot_nt(s["rg"][...], proj).astype(BF)
        s["hs"][2 * pair] = grads[:, 0:VD]
        s["hs"][2 * pair + 1] = grads[:, VD : 2 * VD]
        for parity in (0, 1):
            if step:
                e = 2 * pair + parity
                send(s["hs"].at[e], s["hr"].at[me], s["s_h"].at[0], s["s_h"].at[1], (ctx, e))
        if not step:
            e = lmate[1]
            send(s["hs"].at[e], s["hr"].at[me], s["s_h"].at[0], s["s_h"].at[1], (ctx, e))
            own_h = pltpu.make_async_copy(s["hs"].at[me], s["hr"].at[me], s["s_local"].at[7])
            own_h.start()

    own_o = []
    for buf in range(2):
        for dev in exps:
            send(os.at[buf, dev[1]], s["orr"].at[buf, me], s["s_o"].at[buf], s["s_o"].at[2 + buf], dev)
        copy = pltpu.make_async_copy(os.at[buf, me], s["orr"].at[buf, me], s["s_local"].at[5 + buf])
        copy.start()
        own_o.append(copy)
    s["dk"][...] = jnp.zeros((QK, REACH + TOK), F32)
    s["dv"][...] = jnp.zeros((REACH + TOK, VD), F32)
    own_h.wait()
    wait(s["hr"].at[pl.ds(0, 7)], s["s_h"].at[1])

    for src in range(N_EXP):
        lead = s["hr"][:, 16 * src : 16 * src + 16, :].reshape(128, VD)
        tail = s["hr"][:, 128 + 16 * (src // 2) : 144 + 16 * (src // 2), :].reshape(128, VD)
        rows = dot_nn(s["tab"][src], jnp.concatenate([lead, tail], axis=0))
        s["grads"][TOK_DEV * src : TOK_DEV * src + TOK_DEV, :] = rows.astype(BF)

    for b in range(N_QB):
        rows, window = pl.ds(QB * b, QB), pl.ds(QB * b, WIN)
        grad = s["grads"][rows, :]
        delta = jnp.sum(grad.astype(F32) * s["att"][rows, :], axis=1, keepdims=True)
        prob_grad = dot_nt(grad, s["vw"][window, :])
        score_grad = (s["probs"][b] * (prob_grad - delta)).astype(BF)
        s["dv"][window, :] += dot_nn(s["plt"][b], grad)
        s["dk"][:, window] += dot_nn(qt[:, rows], score_grad)
        out_q[:, rows] = (dot_nt(s["kw"][:, window], score_grad) * SCALE).astype(BF)
        if b == 1:
            s["ks"][...] = (s["dk"][:, 0:REACH] * SCALE).astype(BF)
            s["vs"][...] = s["dv"][0:REACH, :].astype(BF)
            send(s["ks"], s["kr"], s["s_k"].at[0], s["s_k"].at[1], before)
            send(s["vs"], s["vr"], s["s_k"].at[2], s["s_k"].at[3], before)
    out_k[:, 0:REACH] = (s["dk"][:, REACH : 2 * REACH] * SCALE).astype(BF)
    out_v[0:REACH, :] = s["dv"][REACH : 2 * REACH, :].astype(BF)
    wait(s["kr"], s["s_k"].at[1])
    out_k[:, REACH:TOK] = (
        s["dk"][:, 2 * REACH : 3 * REACH] * SCALE + s["kr"][...].astype(F32)
    ).astype(BF)
    wait(s["vr"], s["s_k"].at[3])
    out_v[REACH:TOK, :] = (s["dv"][2 * REACH : 3 * REACH, :] + s["vr"][...].astype(F32)).astype(BF)

    for buf in range(2):
        own_o[buf].wait()
        wait(s["orr"].at[buf, pl.ds(0, 7)], s["s_o"].at[2 + buf])
        got = s["orr"][buf].reshape(N_EXP * SLOTS, 512)
        out_res[:, 1024 * buf : 1024 * buf + 512] = dot_nn(s["tin"][...], got).astype(BF)
        out_res[:, 1024 * buf + 512 : 1024 * buf + 1024] = dot_nn(s["tdy"][...], got).astype(BF)

    wait(s["w"].at[pl.ds(0, 63)], s["s_wsend"])
    wait(s["opf"].at[pl.ds(0, 7)], s["s_op_s"])
    wait(keys_in.at[:, pl.ds(0, REACH)], s["s_halo_s"].at[0])
    wait(values_in.at[pl.ds(0, REACH)], s["s_halo_s"].at[1])
    wait(s["segh"], s["s_halo_s"].at[2])
    wait(s["xs"].at[pl.ds(0, 7)], s["s_x"].at[0])
    wait(s["auxs"].at[pl.ds(0, 7)], s["s_aux"].at[0])
    wait(s["placer"].at[pl.ds(0, 7)], s["s_aux"].at[2])
    for buf in range(2):
        wait(os.at[buf, pl.ds(0, 7)], s["s_o"].at[buf])
    wait(s["hs"].at[pl.ds(0, 7)], s["s_h"].at[0])
    wait(s["ks"], s["s_k"].at[0])
    wait(s["vs"], s["s_k"].at[2])


def shards(
    residual, out_grad, norm_gain, expert_ids, route_weights, gate_up, down_proj, out_proj,
    queries, keys_in, values_in, segments,
):
    vm = pl.BlockSpec(memory_space=pltpu.VMEM)
    hbm = pl.BlockSpec(memory_space=pl.ANY)
    residual_grad, query_grad, key_grad, value_grad = pl.pallas_call(
        body,
        out_shape=(
            jax.ShapeDtypeStruct((TOK_DEV, D), BF),
            jax.ShapeDtypeStruct((QK, TOK), BF),
            jax.ShapeDtypeStruct((QK, TOK), BF),
            jax.ShapeDtypeStruct((TOK, VD), BF),
        ),
        in_specs=[hbm] * 4 + [vm] * 8,
        out_specs=(vm,) * 4,
        scratch_shapes=list(scratch().values()),
        compiler_params=pltpu.CompilerParams(
            collective_id=0, has_side_effects=True, vmem_limit_bytes=60 * 1024 * 1024
        ),
    )(
        gate_up.reshape(64, FF), out_proj, keys_in.T, values_in, down_proj.reshape(12, D),
        residual, out_grad, norm_gain.reshape(16, 128), expert_ids.T, route_weights.T,
        segments.reshape(8, 128), queries.T,
    )
    return residual_grad, query_grad.T, key_grad.T, value_grad


def solution(mesh):
    return jax.shard_map(
        shards,
        mesh=mesh,
        in_specs=(
            P(("ctx", "exp"), None),
            P(("ctx", "exp"), None),
            P(),
            P(("ctx", "exp"), None),
            P(("ctx", "exp"), None),
            P("exp", None, "ctx", None),
            P("exp", "ctx", None),
            P("exp", None),
            P("ctx", "exp"),
            P("ctx", "exp"),
            P("ctx", "exp"),
            P("ctx"),
        ),
        out_specs=(P(("ctx", "exp"), None), P("ctx", "exp"), P("ctx", "exp"), P("ctx", "exp")),
        check_vma=False,
    )
```

```python
import functools

import jax
import jax.numpy as jnp
from jax import lax
from jax.experimental import pallas as pl
from jax.experimental.pallas import tpu as pltpu
from jax.sharding import PartitionSpec as P

D = 2048
QK = 192
VD = 128
FF = 768
TOPK = 6
N_EXP = 8
N_CTX = 64
NH = 4
NY = 8
TOK = 1024
REACH = 512
TOK_DEV = 128
CAP = 24
SLOTS = 48
LIVE = N_EXP * CAP
SHARD = 96
QB = 256
WIN = QB + REACH
N_QB = TOK // QB
EPSILON = 1e-06
MASKED = -1e30
SCALE = QK ** (-0.5)
BF = jnp.bfloat16
F32 = jnp.float32
MESH = pl.DeviceIdType.MESH


def dot_nn(a, b):
    return lax.dot_general(a, b, (((1,), (0,)), ((), ())), preferred_element_type=F32)


def dot_nt(a, b):
    return lax.dot_general(a, b, (((1,), (1,)), ((), ())), preferred_element_type=F32)


def dot_tn(a, b):
    return lax.dot_general(a, b, (((0,), (0,)), ((), ())), preferred_element_type=F32)


def scratch():
    vm, dma = pltpu.VMEM, pltpu.SemaphoreType.DMA
    return dict(
        w=vm((N_CTX, SHARD, FF), BF),
        opf=vm((N_EXP, VD, D), BF),
        lhs=vm((2 * TOK_DEV, D), BF),
        xs=vm((N_EXP, SLOTS, D), BF),
        xr=vm((N_EXP, SLOTS, D), BF),
        sel=vm((NH, 2, 256, FF), BF),
        pre=vm((256, 2 * FF), F32),
        hid=vm((256, FF), F32),
        gg=vm((LIVE, 2 * FF), BF),
        os=vm((2, N_EXP, SLOTS, 512), BF),
        orr=vm((2, N_EXP, SLOTS, 512), BF),
        tin=vm((TOK_DEV, N_EXP * SLOTS), BF),
        tdy=vm((TOK_DEV, N_EXP * SLOTS), BF),
        inv=vm((TOK_DEV, 1), F32),
        auxs=vm((N_EXP, CAP, 128), F32),
        auxr=vm((N_EXP, CAP, 128), F32),
        places=vm((8, 128), jnp.int32),
        placer=vm((N_EXP, 8, 128), jnp.int32),
        tab=vm((N_EXP, TOK_DEV, 256), BF),
        ng=vm((LIVE, D), F32),
        rg=vm((LIVE, D), BF),
        hs=vm((N_EXP, LIVE, VD), BF),
        hr=vm((N_EXP, LIVE, VD), BF),
        grads=vm((TOK, VD), BF),
        kw=vm((QK, REACH + TOK), BF),
        vw=vm((REACH + TOK, VD), BF),
        segh=vm((8, 128), jnp.int32),
        probs=vm((N_QB, QB, WIN), F32),
        plt=vm((N_QB, WIN, QB), BF),
        att=vm((TOK, VD), F32),
        dk=vm((QK, REACH + TOK), F32),
        dv=vm((REACH + TOK, VD), F32),
        ks=vm((2, QK, QB), BF),
        vs=vm((2, QB, VD), BF),
        kr=vm((2, QK, QB), BF),
        vr=vm((2, QB, VD), BF),
        s_local=dma((10,)),
        s_wsend=dma,
        s_z=dma((2,)),
        s_half=dma((2,)),
        s_w=dma((NH * NY,)),
        s_cross=dma((NH,)),
        s_halo_s=dma((3,)),
        s_halo_r=dma((3,)),
        s_op_s=dma,
        s_op_r=dma((4,)),
        s_x=dma((2,)),
        s_aux=dma((4,)),
        s_o=dma((4,)),
        s_h=dma((2,)),
        s_k=dma((8,)),
    )


NAMES = tuple(scratch())


def body(
    gu_in, op_in, keys_in, values_in, down_in, res, dy, gain, ids, rw, seg, qt,
    out_res, out_q, out_k, out_v, *rest,
):
    s = dict(zip(NAMES, rest))
    ctx, me = lax.axis_index("ctx"), lax.axis_index("exp")
    h, y, c = ctx // 16, (ctx // 2) % NY, ctx % 2
    x, l = me // 2, me % 2

    def at(hh, yy):
        return (hh * NY + yy) * 2 + c

    sibling = (ctx + 1 - 2 * c, me)
    up = (at(h, (y + 1) % NY), me)
    down = (at(h, (y + NY - 1) % NY), me)
    zs = [(at((h + k) % NH, y), me) for k in range(1, NH)]
    after = ((ctx + 1) % N_CTX, me)
    before = ((ctx + N_CTX - 1) % N_CTX, me)
    exps = [(ctx, (me + k) % N_EXP) for k in range(1, N_EXP)]
    lmate = (ctx, 2 * x + 1 - l)
    xmates = [(ctx, 2 * ((x + k) % 4) + l) for k in (2, 1, 3)]

    def send(src, dst, ssem, rsem, dev):
        pltpu.make_async_remote_copy(
            src_ref=src, dst_ref=dst, send_sem=ssem, recv_sem=rsem,
            device_id=dev, device_id_type=MESH,
        ).start()

    def wait(ref, sem):
        pltpu.make_async_copy(ref, ref, sem).wait()

    partners = [sibling, up, down, after, before] + zs + exps
    barrier = pltpu.get_barrier_semaphore()
    for dev in partners:
        pl.semaphore_signal(barrier, inc=1, device_id=dev, device_id_type=MESH)
    local = [
        pltpu.make_async_copy(gu_in, s["w"].at[ctx, pl.ds(0, 64)], s["s_local"].at[0]),
        pltpu.make_async_copy(op_in, s["opf"].at[me], s["s_local"].at[1]),
        pltpu.make_async_copy(keys_in, s["kw"].at[:, pl.ds(REACH, TOK)], s["s_local"].at[2]),
        pltpu.make_async_copy(values_in, s["vw"].at[pl.ds(REACH, TOK)], s["s_local"].at[3]),
    ]
    for copy in local:
        copy.start()
    rows12 = down_in[...].astype(F32)
    tail = [
        jnp.concatenate([rows12[3 * a + b : 3 * a + b + 1, 1536:2048] for a in range(4)], axis=0)
        for b in range(3)
    ]
    rows16 = jnp.concatenate([rows12[:, 0:1536], jnp.concatenate(tail, axis=1)], axis=0).astype(BF)
    s["w"][ctx, 64:80, :] = rows16[:, 0:768]
    s["w"][ctx, 80:96, :] = rows16[:, 768:1536]
    local[0].wait()
    w_in = s["w"].at[ctx]
    pl.semaphore_wait(barrier, len(partners))

    def wsend(src, hh, yy, dev, sem=None):
        j = at(hh, yy)
        send(src, s["w"].at[j], s["s_wsend"] if sem is None else sem, s["s_w"].at[hh * NY + yy], dev)

    def cross(src, hh, yy):
        send(src, s["w"].at[at(hh, yy)], s["s_wsend"], s["s_cross"].at[hh], sibling)

    wsend(w_in, h, y, up)
    wsend(w_in, h, y, down)
    wsend(w_in, h, y, zs[0], s["s_z"].at[0])
    wsend(w_in, h, y, zs[2], s["s_z"].at[1])
    cross(w_in, h, y)
    half = pl.ds(64 * c, 64)
    send(op_in.at[half], s["opf"].at[me, half], s["s_op_s"], s["s_op_r"].at[0], lmate)
    for dev in xmates:
        send(op_in.at[half], s["opf"].at[me, half], s["s_op_s"], s["s_op_r"].at[1], dev)
    send(keys_in.at[:, pl.ds(REACH, REACH)], s["kw"].at[:, pl.ds(0, REACH)],
         s["s_halo_s"].at[0], s["s_halo_r"].at[0], after)
    send(values_in.at[pl.ds(REACH, REACH)], s["vw"].at[pl.ds(0, REACH)],
         s["s_halo_s"].at[1], s["s_halo_r"].at[1], after)
    send(seg, s["segh"], s["s_halo_s"].at[2], s["s_halo_r"].at[2], after)

    gain_rows = gain[...].astype(F32)
    gain_f = jnp.concatenate([gain_rows[i : i + 1, :] for i in range(16)], axis=1)

    def normalize():
        for r in range(0, TOK_DEV, 16):
            rows = pl.ds(r, 16)
            feats = res[rows, :].astype(F32)
            inverse = lax.rsqrt(jnp.mean(feats * feats, axis=1, keepdims=True) + EPSILON)
            s["inv"][rows, :] = inverse
            s["lhs"][rows, :] = (feats * inverse * gain_f).astype(BF)
        s["lhs"][pl.ds(TOK_DEV, TOK_DEV), :] = dy[...]

    ids_v = ids[...]
    live = ids_v < N_EXP
    expert = jnp.sum(jnp.where(live, ids_v, 0), axis=0, keepdims=True)
    first = lax.broadcasted_iota(jnp.int32, (TOK_DEV, TOK_DEV), 0)
    second = lax.broadcasted_iota(jnp.int32, (TOK_DEV, TOK_DEV), 1)
    earlier = jnp.where(first < second, 1.0, 0.0).astype(BF)
    onehot = jnp.where(lax.broadcasted_iota(jnp.int32, (16, TOK_DEV), 0) == expert, 1.0, 0.0)
    counts = dot_nn(onehot.astype(BF), earlier)
    rank = jnp.sum(onehot * counts, axis=0, keepdims=True).astype(jnp.int32)
    place_in = expert * SLOTS + jnp.where(rank < 16, rank, rank + 16)
    place_dy = expert * SLOTS + jnp.where(rank < 16, rank + 16, rank + 24)
    slot = lax.broadcasted_iota(jnp.int32, (N_EXP * SLOTS, TOK_DEV), 0)
    hit_in = jnp.where(slot == place_in, 1.0, 0.0).astype(BF)
    hit_dy = jnp.where(slot == place_dy, 1.0, 0.0).astype(BF)

    def dispatch(*columns):
        table = jnp.concatenate([hit_in, hit_dy], axis=1)
        for col in columns:
            picked = dot_nn(table, s["lhs"][:, col : col + 512])
            s["xs"][:, :, col : col + 512] = picked.astype(BF).reshape(N_EXP, SLOTS, 512)

    own = [
        pltpu.make_async_copy(s["xs"].at[me], s["xr"].at[me], s["s_local"].at[4]),
        pltpu.make_async_copy(s["auxs"].at[me], s["auxr"].at[me], s["s_local"].at[8]),
        pltpu.make_async_copy(s["places"], s["placer"].at[me], s["s_local"].at[9]),
    ]

    def dispatch_send():
        for dev in exps:
            send(s["xs"].at[dev[1]], s["xr"].at[me], s["s_x"].at[0], s["s_x"].at[1], dev)
        own[0].start()

    def side_send():
        weight = jnp.sum(jnp.where(live, rw[...].astype(F32), 0.0), axis=0, keepdims=True)
        weight = jnp.transpose(jnp.broadcast_to(weight, (8, TOK_DEV)))[:, 0:1]
        inverse = s["inv"][...]
        high = inverse.astype(BF).astype(F32)
        mid = (inverse - high).astype(BF).astype(F32)
        low = inverse - high - mid
        lane = lax.broadcasted_iota(jnp.int32, (TOK_DEV, 128), 1)
        terms = jnp.where(lane == 0, high, jnp.where(lane == 1, mid, jnp.where(lane == 2, low, jnp.where(lane == 3, weight, 0.0))))
        picked = dot_nn(hit_in, terms.astype(BF)).reshape(N_EXP, SLOTS, 128)
        s["auxs"][:, 0:16, :] = picked[:, 0:16]
        s["auxs"][:, 16:24, :] = picked[:, 32:40]
        code = expert * 16 + jnp.where(rank < 16, rank, rank + 112 + 8 * (me % 2))
        s["places"][...] = jnp.broadcast_to(code, (8, 128))
        for dev in exps:
            send(s["auxs"].at[dev[1]], s["auxr"].at[me], s["s_aux"].at[0], s["s_aux"].at[1], dev)
            send(s["places"], s["placer"].at[me], s["s_aux"].at[2], s["s_aux"].at[3], dev)
        own[1].start()
        own[2].start()

    def tables():
        s["tin"][...] = jnp.transpose(hit_in)
        s["tdy"][...] = jnp.transpose(hit_dy)

    def clear():
        s["dk"][...] = jnp.zeros((QK, REACH + TOK), F32)
        s["dv"][...] = jnp.zeros((REACH + TOK, VD), F32)

    def places_ready():
        own[2].wait()
        wait(s["placer"].at[pl.ds(0, 7)], s["s_aux"].at[3])

    def place_table(src):
        at_row = lax.broadcasted_iota(jnp.int32, (256, TOK_DEV), 0) == s["placer"][src, 0:1, :]
        s["tab"][src] = jnp.transpose(jnp.where(at_row, 1.0, 0.0).astype(BF))

    def rows_ready():
        own[0].wait()
        own[1].wait()
        wait(s["xr"].at[pl.ds(0, 7)], s["s_x"].at[1])
        wait(s["auxr"].at[pl.ds(0, 7)], s["s_aux"].at[1])

    def selection(k):
        hh = (h + k) % NH
        i = lax.broadcasted_iota(jnp.int32, (256, FF), 0)
        f = lax.broadcasted_iota(jnp.int32, (256, FF), 1)
        m = i % 16
        base = 192 * hh + 12 * (i // 16)
        first = base + jnp.where(m < 12, m, 3 * (m - 12))
        second = base + jnp.where(m >= 12, 3 * (m - 12) + 1, jnp.where(m >= 8, 3 * (m - 8) + 2, -9999))
        s["sel"][k, 0] = jnp.where(f == first, 1.0, 0.0).astype(BF)
        s["sel"][k, 1] = jnp.where(f == second, 1.0, 0.0).astype(BF)

    def halo_ready():
        wait(s["kw"].at[:, pl.ds(0, REACH)], s["s_halo_r"].at[0])
        wait(s["vw"].at[pl.ds(0, REACH)], s["s_halo_r"].at[1])
        wait(s["segh"], s["s_halo_r"].at[2])
        local[2].wait()
        local[3].wait()

    def seg_row(r):
        return s["segh"][4 + r : 5 + r, :] if r < 4 else seg[r - 4 : r - 3, :]

    def forward(b):
        seg_cols = jnp.transpose(seg[...].astype(F32)).astype(jnp.int32)
        seg_q = jnp.concatenate([seg_cols[:, 2 * b : 2 * b + 1], seg_cols[:, 2 * b + 1 : 2 * b + 2]], axis=0)
        pos_q = lax.broadcasted_iota(jnp.int32, (QB, 128), 0) + REACH
        pos_k = lax.broadcasted_iota(jnp.int32, (QB, 128), 1)
        scores = dot_nn(jnp.transpose(qt[:, pl.ds(QB * b, QB)]), s["kw"][:, pl.ds(QB * b, WIN)]) * SCALE
        pieces = []
        for t in range(WIN // 128):
            allowed = (seg_q == seg_row(2 * b + t)) & (pos_k + 128 * t <= pos_q)
            if 2 * b + t < 4:
                allowed = allowed & (ctx > 0)
            pieces.append(jnp.where(allowed, scores[:, 128 * t : 128 * t + 128], MASKED))
        scores = jnp.concatenate(pieces, axis=1)
        top = jnp.max(scores, axis=1, keepdims=True)
        raw = jnp.exp(scores - top)
        probs = raw / jnp.sum(raw, axis=1, keepdims=True)
        low = probs.astype(BF)
        s["probs"][b] = probs
        s["plt"][b] = jnp.transpose(low)
        s["att"][pl.ds(QB * b, QB), :] = (
            dot_nn(low, s["vw"][pl.ds(QB * b, WIN), :]).astype(BF).astype(F32)
        )

    def op_pass():
        wait(s["opf"].at[0, pl.ds(0, 64)], s["s_op_r"].at[0])
        other = lmate[1]
        for dev in xmates:
            send(s["opf"].at[other, half], s["opf"].at[other, half], s["s_op_s"], s["s_op_r"].at[2], dev)
        send(s["opf"].at[other, half], s["opf"].at[other, half], s["s_op_s"], s["s_op_r"].at[3], sibling)

    def op_cross(k, parity):
        wait(s["opf"].at[pl.ds(0, 3), pl.ds(0, 64)], s["s_op_r"].at[k])
        for step in (1, 2, 3):
            e = 2 * ((x + step) % 4) + parity
            send(s["opf"].at[e, half], s["opf"].at[e, half], s["s_op_s"], s["s_op_r"].at[3], sibling)

    def arrive(d, k, way):
        hh = (h + k) % NH
        yy = (y + NY - way * d) % NY
        j = at(hh, yy)
        src = s["w"].at[j]
        if d == 4 and k == 1:
            for part in range(2):
                wait(s["w"].at[0, pl.ds(0, 48)], s["s_half"].at[part])
        else:
            wait(s["w"].at[0], s["s_w"].at[hh * NY + yy])
        if d == 0:
            wsend(src, hh, yy, up)
            wsend(src, hh, yy, down)
        elif d < 3 or (d == 3 and k != 1 and (k == 0) == (way == 1)):
            wsend(src, hh, yy, up if way == 1 else down)
        elif d == 3 and k == 1:
            part = 0 if way == 1 else 1
            rows = pl.ds(48 * part, 48)
            send(src.at[rows], s["w"].at[j, rows], s["s_wsend"], s["s_half"].at[part], up if way == 1 else down)
        cross(src, hh, yy)

    def far_send():
        wait(s["w"].at[0], s["s_z"].at[0])
        wait(s["w"].at[0], s["s_z"].at[1])
        wsend(w_in, h, y, zs[1])

    def experts(k):
        hh = (h + k) % NH
        wait(s["w"].at[pl.ds(0, NY)], s["s_cross"].at[hh])
        block = pl.ds(16 * hh, 16)
        cols = pl.ds(pl.multiple_of(512 * hh, 512), 512)
        xr, w = s["xr"], s["w"]

        def stacked(first, columns):
            lead = xr[:, first : first + 16, columns].reshape(128, -1)
            tail = xr[:, 32:48, columns].reshape(128, -1)
            return jnp.concatenate([lead, tail], axis=0)

        rows_in = stacked(0, cols)
        gate = dot_nn(rows_in, w[block, 0:32, :].reshape(512, FF))
        upper = dot_nn(rows_in, w[block, 32:64, :].reshape(512, FF))
        if k == 0:
            s["pre"][:, 0:FF] = gate
            s["pre"][:, FF : 2 * FF] = upper
        else:
            s["pre"][:, 0:FF] += gate
            s["pre"][:, FF : 2 * FF] += upper
        d0 = w[block, 64:80, :].reshape(256, FF)
        d1 = w[block, 80:96, :].reshape(256, FF)
        h0 = dot_nt(stacked(16, slice(0, 768)), d0) + dot_nt(stacked(16, slice(768, 1536)), d1)
        last = stacked(16, slice(1536, 2048))
        h1 = dot_nt(last, d0[:, 0:512])
        h2 = dot_nt(last[:, 0:256], d0[:, 512:768]) + dot_nt(last[:, 256:512], d1[:, 0:256])
        h3 = dot_nt(last, d1[:, 256:768])
        m = lax.broadcasted_iota(jnp.int32, (256, 256), 1) % 16
        z1 = jnp.where(m < 12, h0, h1)
        z2 = jnp.where(m < 12, pltpu.roll(h3, 252, 1), h2)
        hid = dot_nn(z1.astype(BF), s["sel"][k, 0]) + dot_nn(z2.astype(BF), s["sel"][k, 1])
        if k == 0:
            s["hid"][...] = hid
        else:
            s["hid"][...] += hid

    normalize()
    steps = [
        (1, 0, -1), (1, 0, 1),
        lambda: dispatch(0, 512), far_send,
        (0, 1, 0), (0, 3, 0),
        lambda: dispatch(1024, 1536), dispatch_send,
        (2, 0, -1), (2, 0, 1),
        side_send,
        (1, 1, -1), (1, 1, 1), (0, 2, 0),
        tables, lambda: selection(0),
        (1, 3, -1), (1, 3, 1),
        lambda: selection(1), op_pass, clear,
        (3, 0, -1), (3, 0, 1),
        halo_ready, lambda: forward(0),
        (2, 1, -1), (2, 1, 1),
        lambda: forward(1),
        (1, 2, -1), (1, 2, 1),
        lambda: forward(2), lambda: op_cross(1, l),
        (2, 3, -1), (2, 3, 1),
        lambda: forward(3),
        (3, 1, -1), (3, 1, 1), (4, 0, 1),
        places_ready, lambda: [place_table(src) for src in range(4)],
        (2, 2, -1), (2, 2, 1),
        lambda: [place_table(src) for src in range(4, 8)], lambda: selection(2),
        (3, 3, -1), (3, 3, 1),
        lambda: selection(3), rows_ready, lambda: experts(0),
        (3, 2, -1), (3, 2, 1),
        lambda: op_cross(2, 1 - l),
        (4, 1, 1), (4, 3, -1),
        lambda: experts(1),
        (4, 2, -1),
        lambda: experts(3), lambda: experts(2),
    ]
    for step in steps:
        if callable(step):
            step()
        else:
            arrive(*step)

    for part in range(6):
        if part < 4:
            rows = slice(32 * part, 32 * part + 32)
            gate = s["pre"][rows, 0:FF]
            upper = s["pre"][rows, FF : 2 * FF]
            hid = s["hid"][rows, :]
        else:
            rows = slice(128 + 64 * (part - 4), 192 + 64 * (part - 4))
            gate = s["pre"][rows, 0:FF].reshape(4, 16, FF)[:, 0:8].reshape(32, FF)
            upper = s["pre"][rows, FF : 2 * FF].reshape(4, 16, FF)[:, 0:8].reshape(32, FF)
            hid = s["hid"][rows, :].reshape(4, 16, FF)[:, 8:16].reshape(32, FF)
        sigm = jax.nn.sigmoid(gate)
        put = pl.ds(32 * part, 32)
        s["gg"][put, 0:FF] = (hid * upper * sigm * (1.0 + gate * (1.0 - sigm))).astype(BF)
        s["gg"][put, FF : 2 * FF] = (hid * gate * sigm).astype(BF)

    gg, os = s["gg"], s["os"]
    xr = s["xr"]
    side = jnp.concatenate(
        [s["auxr"][:, 0:16, :].reshape(128, 128), s["auxr"][:, 16:24, :].reshape(64, 128)], axis=0
    )
    inverse = side[:, 0:1] + side[:, 1:2] + side[:, 2:3]
    weight = side[:, 3:4]

    def slot_rows(first, cols):
        lead = xr[:, 16 * first : 16 * first + 16, cols].reshape(128, -1).astype(F32)
        tail = xr[:, 32:48, cols].astype(F32)[:, 8 * first : 8 * first + 8].reshape(64, -1)
        return jnp.concatenate([lead, tail], axis=0)

    dots = jnp.zeros((LIVE, 128), F32)
    for n in range(8):
        block, cols = pl.ds(8 * n, 8), pl.ds(256 * n, 256)
        grad = weight * (
            dot_nt(gg[:, 0:FF], s["w"][block, 0:32, :].reshape(256, FF))
            + dot_nt(gg[:, FF : 2 * FF], s["w"][block, 32:64, :].reshape(256, FF))
        )
        s["ng"][:, cols] = grad
        prod = grad * slot_rows(0, cols)
        dots = dots + prod[:, 0:128] + prod[:, 128:256]
    share = inverse * (jnp.sum(dots, axis=1, keepdims=True) / D)
    gain_inv = 1.0 / gain_f

    def total(n):
        cols = pl.ds(256 * n, 256)
        lanes = slice(256 * n, 256 * n + 256)
        value = (
            slot_rows(1, cols)
            + inverse * (s["ng"][:, cols] * gain_f[:, lanes])
            - slot_rows(0, cols) * share * gain_inv[:, lanes]
        )
        s["rg"][:, cols] = value.astype(BF)
        return value

    for buf in range(2):
        for sub in range(2):
            cols = pl.ds(256 * sub, 256)
            o0 = total(4 * buf + sub)
            o1 = total(4 * buf + 2 + sub)
            os[buf, :, 0:16, cols] = o0[0:128].astype(BF).reshape(N_EXP, 16, 256)
            os[buf, :, 16:32, cols] = o1[0:128].astype(BF).reshape(N_EXP, 16, 256)
            tail = jnp.concatenate(
                [o0[128:192].reshape(N_EXP, 8, 256), o1[128:192].reshape(N_EXP, 8, 256)], axis=1
            )
            os[buf, :, 32:48, cols] = tail.astype(BF)

    def home_send(buf, e):
        send(os.at[buf, e], s["orr"].at[buf, me], s["s_o"].at[buf], s["s_o"].at[2 + buf], (ctx, e))

    home_send(0, 2 * ((x + 2) % 4))
    home_send(0, 2 * ((x + 2) % 4) + 1)

    local[1].wait()
    wait(s["opf"].at[pl.ds(0, 7), pl.ds(0, 64)], s["s_op_r"].at[3])
    own_h = None
    for step in (2, 1, 3, 0):
        pair = (x + step) % 4
        proj = s["opf"][pl.ds(2 * pair, 2)].reshape(2 * VD, D)
        grads = dot_nt(s["rg"][...], proj).astype(BF)
        s["hs"][2 * pair] = grads[:, 0:VD]
        s["hs"][2 * pair + 1] = grads[:, VD : 2 * VD]
        for parity in (0, 1):
            if step:
                e = 2 * pair + parity
                send(s["hs"].at[e], s["hr"].at[me], s["s_h"].at[0], s["s_h"].at[1], (ctx, e))
        if not step:
            e = lmate[1]
            send(s["hs"].at[e], s["hr"].at[me], s["s_h"].at[0], s["s_h"].at[1], (ctx, e))
            own_h = pltpu.make_async_copy(s["hs"].at[me], s["hr"].at[me], s["s_local"].at[7])
            own_h.start()


    wait(s["hs"].at[pl.ds(0, 7)], s["s_h"].at[0])
    own_o = []
    for buf in range(2):
        for step in (2, 1, 3, 0):
            for e in (2 * ((x + step) % 4), 2 * ((x + step) % 4) + 1) if step else (lmate[1],):
                if buf or step != 2:
                    home_send(buf, e)
        copy = pltpu.make_async_copy(os.at[buf, me], s["orr"].at[buf, me], s["s_local"].at[5 + buf])
        copy.start()
        own_o.append(copy)
    own_h.wait()
    wait(s["hr"].at[pl.ds(0, 7)], s["s_h"].at[1])

    for src in range(N_EXP):
        lead = s["hr"][:, 16 * src : 16 * src + 16, :].reshape(128, VD)
        tail = s["hr"][:, 128 + 16 * (src // 2) : 144 + 16 * (src // 2), :].reshape(128, VD)
        rows = dot_nn(s["tab"][src], jnp.concatenate([lead, tail], axis=0))
        s["grads"][TOK_DEV * src : TOK_DEV * src + TOK_DEV, :] = rows.astype(BF)

    for b in range(N_QB):
        rows, window = pl.ds(QB * b, QB), pl.ds(QB * b, WIN)
        grad = s["grads"][rows, :]
        delta = jnp.sum(grad.astype(F32) * s["att"][rows, :], axis=1, keepdims=True)
        prob_grad = dot_nt(grad, s["vw"][window, :])
        score_grad = (s["probs"][b] * (prob_grad - delta)).astype(BF)
        s["dv"][window, :] += dot_nn(s["plt"][b], grad)
        s["dk"][:, window] += dot_nn(qt[:, rows], score_grad)
        out_q[:, rows] = (dot_nt(s["kw"][:, window], score_grad) * SCALE).astype(BF)
        if b < 2:
            s["ks"][b] = (s["dk"][:, rows] * SCALE).astype(BF)
            s["vs"][b] = s["dv"][rows, :].astype(BF)
            send(s["ks"].at[b], s["kr"].at[b], s["s_k"].at[b], s["s_k"].at[2 + b], before)
            send(s["vs"].at[b], s["vr"].at[b], s["s_k"].at[4 + b], s["s_k"].at[6 + b], before)
    out_k[:, 0:REACH] = (s["dk"][:, REACH : 2 * REACH] * SCALE).astype(BF)
    out_v[0:REACH, :] = s["dv"][REACH : 2 * REACH, :].astype(BF)
    for b in range(2):
        rows, mine = pl.ds(REACH + QB * b, QB), pl.ds(2 * REACH + QB * b, QB)
        wait(s["kr"].at[b], s["s_k"].at[2 + b])
        out_k[:, rows] = (s["dk"][:, mine] * SCALE + s["kr"][b].astype(F32)).astype(BF)
        wait(s["vr"].at[b], s["s_k"].at[6 + b])
        out_v[rows, :] = (s["dv"][mine, :] + s["vr"][b].astype(F32)).astype(BF)
    for buf in range(2):
        own_o[buf].wait()
        wait(s["orr"].at[buf, pl.ds(0, 7)], s["s_o"].at[2 + buf])
        got = s["orr"][buf].reshape(N_EXP * SLOTS, 512)
        out_res[:, 1024 * buf : 1024 * buf + 512] = dot_nn(s["tin"][...], got).astype(BF)
        out_res[:, 1024 * buf + 512 : 1024 * buf + 1024] = dot_nn(s["tdy"][...], got).astype(BF)

    wait(s["w"].at[pl.ds(0, 61)], s["s_wsend"])
    wait(s["opf"].at[pl.ds(0, 7)], s["s_op_s"])
    wait(keys_in.at[:, pl.ds(0, REACH)], s["s_halo_s"].at[0])
    wait(values_in.at[pl.ds(0, REACH)], s["s_halo_s"].at[1])
    wait(s["segh"], s["s_halo_s"].at[2])
    wait(s["xs"].at[pl.ds(0, 7)], s["s_x"].at[0])
    wait(s["auxs"].at[pl.ds(0, 7)], s["s_aux"].at[0])
    wait(s["placer"].at[pl.ds(0, 7)], s["s_aux"].at[2])
    for buf in range(2):
        wait(os.at[buf, pl.ds(0, 7)], s["s_o"].at[buf])
    for b in range(2):
        wait(s["ks"].at[b], s["s_k"].at[b])
        wait(s["vs"].at[b], s["s_k"].at[4 + b])


def hand_over(a, b, c, d, oa, ob, oc, od, va, vb, vc, vd, sem):
    triples = ((a, va, oa), (b, vb, ob), (c, vc, oc), (d, vd, od))
    into = [pltpu.make_async_copy(t[0], t[1], sem.at[i]) for i, t in enumerate(triples)]
    out = [pltpu.make_async_copy(t[1], t[2], sem.at[4 + i]) for i, t in enumerate(triples)]
    for copy in into:
        copy.start()
    for i in range(4):
        into[i].wait()
        out[i].start()
    for copy in out:
        copy.wait()


def shards(
    residual, out_grad, norm_gain, expert_ids, route_weights, gate_up, down_proj, out_proj,
    queries, keys_in, values_in, segments,
):
    vm = pl.BlockSpec(memory_space=pltpu.VMEM)
    hbm = pl.BlockSpec(memory_space=pl.ANY)
    results = pl.pallas_call(
        body,
        out_shape=(
            jax.ShapeDtypeStruct((TOK_DEV, D), BF),
            jax.ShapeDtypeStruct((QK, TOK), BF),
            jax.ShapeDtypeStruct((QK, TOK), BF),
            jax.ShapeDtypeStruct((TOK, VD), BF),
        ),
        in_specs=[hbm] * 4 + [vm] * 8,
        out_specs=(vm,) * 4,
        scratch_shapes=list(scratch().values()),
        compiler_params=pltpu.CompilerParams(
            collective_id=0, has_side_effects=True, vmem_limit_bytes=60 * 1024 * 1024
        ),
    )(
        gate_up.reshape(64, FF), out_proj, keys_in.T, values_in, down_proj.reshape(12, D),
        residual, out_grad, norm_gain.reshape(16, 128), expert_ids.T, route_weights.T,
        segments.reshape(8, 128), queries.T,
    )
    residual_grad, query_grad, key_grad, value_grad = pl.pallas_call(
        hand_over,
        out_shape=tuple(jax.ShapeDtypeStruct(r.shape, r.dtype) for r in results),
        in_specs=[hbm] * 4,
        out_specs=(hbm,) * 4,
        scratch_shapes=[pltpu.VMEM(r.shape, r.dtype) for r in results] + [pltpu.SemaphoreType.DMA((8,))],
    )(*results)
    return residual_grad, query_grad.T, key_grad.T, value_grad


def solution(mesh):
    return jax.shard_map(
        shards,
        mesh=mesh,
        in_specs=(
            P(("ctx", "exp"), None),
            P(("ctx", "exp"), None),
            P(),
            P(("ctx", "exp"), None),
            P(("ctx", "exp"), None),
            P("exp", None, "ctx", None),
            P("exp", "ctx", None),
            P("exp", None),
            P("ctx", "exp"),
            P("ctx", "exp"),
            P("ctx", "exp"),
            P("ctx"),
        ),
        out_specs=(P(("ctx", "exp"), None), P("ctx", "exp"), P("ctx", "exp"), P("ctx", "exp")),
        check_vma=False,
    )
```

```python
import functools

import jax
import jax.numpy as jnp
from jax import lax
from jax.experimental import pallas as pl
from jax.experimental.pallas import tpu as pltpu
from jax.sharding import PartitionSpec as P

D = 2048
QK = 192
VD = 128
FF = 768
TOPK = 6
N_EXP = 8
N_CTX = 64
NH = 4
NY = 8
TOK = 1024
REACH = 512
TOK_DEV = 128
CAP = 24
SLOTS = 48
LIVE = N_EXP * CAP
SHARD = 96
QB = 256
WIN = QB + REACH
N_QB = TOK // QB
EPSILON = 1e-06
MASKED = -1e30
SCALE = QK ** (-0.5)
BF = jnp.bfloat16
F32 = jnp.float32
MESH = pl.DeviceIdType.MESH


def dot_nn(a, b):
    return lax.dot_general(a, b, (((1,), (0,)), ((), ())), preferred_element_type=F32)


def dot_nt(a, b):
    return lax.dot_general(a, b, (((1,), (1,)), ((), ())), preferred_element_type=F32)


def dot_tn(a, b):
    return lax.dot_general(a, b, (((0,), (0,)), ((), ())), preferred_element_type=F32)


def scratch():
    vm, dma = pltpu.VMEM, pltpu.SemaphoreType.DMA
    return dict(
        w=vm((N_CTX, SHARD, FF), BF),
        opf=vm((N_EXP, VD, D), BF),
        lhs=vm((2 * TOK_DEV, D), BF),
        xs=vm((N_EXP, SLOTS, D), BF),
        xr=vm((N_EXP, SLOTS, D), BF),
        sel=vm((NH, 2, 256, FF), BF),
        pre=vm((256, 2 * FF), F32),
        hid=vm((256, FF), F32),
        gg=vm((LIVE, 2 * FF), BF),
        os=vm((2, N_EXP, SLOTS, 512), BF),
        orr=vm((2, N_EXP, SLOTS, 512), BF),
        tin=vm((TOK_DEV, N_EXP * SLOTS), BF),
        tdy=vm((TOK_DEV, N_EXP * SLOTS), BF),
        inv=vm((TOK_DEV, 1), F32),
        auxs=vm((N_EXP, CAP, 128), F32),
        auxr=vm((N_EXP, CAP, 128), F32),
        places=vm((8, 128), jnp.int32),
        placer=vm((N_EXP, 8, 128), jnp.int32),
        tab=vm((N_EXP, TOK_DEV, 256), BF),
        ng=vm((LIVE, D), F32),
        rg=vm((LIVE, D), BF),
        hs=vm((N_EXP, LIVE, VD), BF),
        hr=vm((N_EXP, LIVE, VD), BF),
        grads=vm((TOK, VD), BF),
        kw=vm((QK, REACH + TOK), BF),
        vw=vm((REACH + TOK, VD), BF),
        segh=vm((8, 128), jnp.int32),
        probs=vm((N_QB, QB, WIN), F32),
        plt=vm((N_QB, WIN, QB), BF),
        att=vm((TOK, VD), F32),
        dk=vm((QK, REACH + TOK), F32),
        dv=vm((REACH + TOK, VD), F32),
        ks=vm((2, QK, QB), BF),
        vs=vm((2, QB, VD), BF),
        kr=vm((2, QK, QB), BF),
        vr=vm((2, QB, VD), BF),
        s_local=dma((10,)),
        s_wsend=dma,
        s_z=dma((2,)),
        s_half=dma((2,)),
        s_w=dma((NH * NY,)),
        s_cross=dma((NH,)),
        s_halo_s=dma((3,)),
        s_halo_r=dma((3,)),
        s_op_s=dma,
        s_op_r=dma((4,)),
        s_x=dma((2,)),
        s_aux=dma((4,)),
        s_o=dma((4,)),
        s_h=dma((2,)),
        s_k=dma((8,)),
    )


NAMES = tuple(scratch())


def body(
    gu_in, op_in, keys_in, values_in, down_in, res, dy, gain, ids, rw, seg, qt,
    out_res, out_q, out_k, out_v, *rest,
):
    s = dict(zip(NAMES, rest))
    ctx, me = lax.axis_index("ctx"), lax.axis_index("exp")
    h, y, c = ctx // 16, (ctx // 2) % NY, ctx % 2
    x, l = me // 2, me % 2

    def at(hh, yy):
        return (hh * NY + yy) * 2 + c

    sibling = (ctx + 1 - 2 * c, me)
    up = (at(h, (y + 1) % NY), me)
    down = (at(h, (y + NY - 1) % NY), me)
    zs = [(at((h + k) % NH, y), me) for k in range(1, NH)]
    after = ((ctx + 1) % N_CTX, me)
    before = ((ctx + N_CTX - 1) % N_CTX, me)
    exps = [(ctx, (me + k) % N_EXP) for k in range(1, N_EXP)]
    lmate = (ctx, 2 * x + 1 - l)
    xmates = [(ctx, 2 * ((x + k) % 4) + l) for k in (2, 1, 3)]

    def send(src, dst, ssem, rsem, dev):
        pltpu.make_async_remote_copy(
            src_ref=src, dst_ref=dst, send_sem=ssem, recv_sem=rsem,
            device_id=dev, device_id_type=MESH,
        ).start()

    def wait(ref, sem):
        pltpu.make_async_copy(ref, ref, sem).wait()

    partners = [sibling, up, down, after, before] + zs + exps
    barrier = pltpu.get_barrier_semaphore()
    for dev in partners:
        pl.semaphore_signal(barrier, inc=1, device_id=dev, device_id_type=MESH)
    local = [
        pltpu.make_async_copy(gu_in, s["w"].at[ctx, pl.ds(0, 64)], s["s_local"].at[0]),
        pltpu.make_async_copy(op_in, s["opf"].at[me], s["s_local"].at[1]),
        pltpu.make_async_copy(keys_in, s["kw"].at[:, pl.ds(REACH, TOK)], s["s_local"].at[2]),
        pltpu.make_async_copy(values_in, s["vw"].at[pl.ds(REACH, TOK)], s["s_local"].at[3]),
    ]
    for copy in local:
        copy.start()
    rows12 = down_in[...].astype(F32)
    tail = [
        jnp.concatenate([rows12[3 * a + b : 3 * a + b + 1, 1536:2048] for a in range(4)], axis=0)
        for b in range(3)
    ]
    rows16 = jnp.concatenate([rows12[:, 0:1536], jnp.concatenate(tail, axis=1)], axis=0).astype(BF)
    s["w"][ctx, 64:80, :] = rows16[:, 0:768]
    s["w"][ctx, 80:96, :] = rows16[:, 768:1536]
    local[0].wait()
    w_in = s["w"].at[ctx]
    pl.semaphore_wait(barrier, len(partners))

    def wsend(src, hh, yy, dev, sem=None):
        j = at(hh, yy)
        send(src, s["w"].at[j], s["s_wsend"] if sem is None else sem, s["s_w"].at[hh * NY + yy], dev)

    def cross(src, hh, yy):
        send(src, s["w"].at[at(hh, yy)], s["s_wsend"], s["s_cross"].at[hh], sibling)

    wsend(w_in, h, y, up)
    wsend(w_in, h, y, down)
    wsend(w_in, h, y, zs[0], s["s_z"].at[0])
    wsend(w_in, h, y, zs[2], s["s_z"].at[1])
    cross(w_in, h, y)
    half = pl.ds(64 * c, 64)
    for dev in xmates:
        send(op_in.at[half], s["opf"].at[me, half], s["s_op_s"], s["s_op_r"].at[1], dev)
    gain_rows = gain[...].astype(F32)
    gain_f = jnp.concatenate([gain_rows[i : i + 1, :] for i in range(16)], axis=1)

    def normalize():
        for r in range(0, TOK_DEV, 16):
            rows = pl.ds(r, 16)
            feats = res[rows, :].astype(F32)
            inverse = lax.rsqrt(jnp.mean(feats * feats, axis=1, keepdims=True) + EPSILON)
            s["inv"][rows, :] = inverse
            s["lhs"][rows, :] = (feats * inverse * gain_f).astype(BF)
        s["lhs"][pl.ds(TOK_DEV, TOK_DEV), :] = dy[...]

    ids_v = ids[...]
    live = ids_v < N_EXP
    expert = jnp.sum(jnp.where(live, ids_v, 0), axis=0, keepdims=True)
    first = lax.broadcasted_iota(jnp.int32, (TOK_DEV, TOK_DEV), 0)
    second = lax.broadcasted_iota(jnp.int32, (TOK_DEV, TOK_DEV), 1)
    earlier = jnp.where(first < second, 1.0, 0.0).astype(BF)
    onehot = jnp.where(lax.broadcasted_iota(jnp.int32, (16, TOK_DEV), 0) == expert, 1.0, 0.0)
    counts = dot_nn(onehot.astype(BF), earlier)
    rank = jnp.sum(onehot * counts, axis=0, keepdims=True).astype(jnp.int32)
    place_in = expert * SLOTS + jnp.where(rank < 16, rank, rank + 16)
    place_dy = expert * SLOTS + jnp.where(rank < 16, rank + 16, rank + 24)
    slot = lax.broadcasted_iota(jnp.int32, (N_EXP * SLOTS, TOK_DEV), 0)
    hit_in = jnp.where(slot == place_in, 1.0, 0.0).astype(BF)
    hit_dy = jnp.where(slot == place_dy, 1.0, 0.0).astype(BF)

    def dispatch(*columns):
        table = jnp.concatenate([hit_in, hit_dy], axis=1)
        for col in columns:
            picked = dot_nn(table, s["lhs"][:, col : col + 512])
            s["xs"][:, :, col : col + 512] = picked.astype(BF).reshape(N_EXP, SLOTS, 512)

    own = [
        pltpu.make_async_copy(s["xs"].at[me], s["xr"].at[me], s["s_local"].at[4]),
        pltpu.make_async_copy(s["auxs"].at[me], s["auxr"].at[me], s["s_local"].at[8]),
        pltpu.make_async_copy(s["places"], s["placer"].at[me], s["s_local"].at[9]),
    ]

    def dispatch_send():
        for dev in exps:
            send(s["xs"].at[dev[1]], s["xr"].at[me], s["s_x"].at[0], s["s_x"].at[1], dev)
        own[0].start()

    def side_send():
        weight = jnp.sum(jnp.where(live, rw[...].astype(F32), 0.0), axis=0, keepdims=True)
        weight = jnp.transpose(jnp.broadcast_to(weight, (8, TOK_DEV)))[:, 0:1]
        inverse = s["inv"][...]
        high = inverse.astype(BF).astype(F32)
        mid = (inverse - high).astype(BF).astype(F32)
        low = inverse - high - mid
        lane = lax.broadcasted_iota(jnp.int32, (TOK_DEV, 128), 1)
        terms = jnp.where(lane == 0, high, jnp.where(lane == 1, mid, jnp.where(lane == 2, low, jnp.where(lane == 3, weight, 0.0))))
        picked = dot_nn(hit_in, terms.astype(BF)).reshape(N_EXP, SLOTS, 128)
        s["auxs"][:, 0:16, :] = picked[:, 0:16]
        s["auxs"][:, 16:24, :] = picked[:, 32:40]
        code = expert * 16 + jnp.where(rank < 16, rank, rank + 112 + 8 * (me % 2))
        s["places"][...] = jnp.broadcast_to(code, (8, 128))
        for dev in exps:
            send(s["auxs"].at[dev[1]], s["auxr"].at[me], s["s_aux"].at[0], s["s_aux"].at[1], dev)
            send(s["places"], s["placer"].at[me], s["s_aux"].at[2], s["s_aux"].at[3], dev)
        own[1].start()
        own[2].start()

    def tables():
        s["tin"][...] = jnp.transpose(hit_in)
        s["tdy"][...] = jnp.transpose(hit_dy)

    def clear():
        s["dk"][...] = jnp.zeros((QK, REACH + TOK), F32)
        s["dv"][...] = jnp.zeros((REACH + TOK, VD), F32)

    def places_ready():
        own[2].wait()
        wait(s["placer"].at[pl.ds(0, 7)], s["s_aux"].at[3])

    def place_table(src):
        at_row = lax.broadcasted_iota(jnp.int32, (256, TOK_DEV), 0) == s["placer"][src, 0:1, :]
        s["tab"][src] = jnp.transpose(jnp.where(at_row, 1.0, 0.0).astype(BF))

    def rows_ready():
        own[0].wait()
        own[1].wait()
        wait(s["xr"].at[pl.ds(0, 7)], s["s_x"].at[1])
        wait(s["auxr"].at[pl.ds(0, 7)], s["s_aux"].at[1])

    def selection(k):
        hh = (h + k) % NH
        i = lax.broadcasted_iota(jnp.int32, (256, FF), 0)
        f = lax.broadcasted_iota(jnp.int32, (256, FF), 1)
        m = i % 16
        base = 192 * hh + 12 * (i // 16)
        first = base + jnp.where(m < 12, m, 3 * (m - 12))
        second = base + jnp.where(m >= 12, 3 * (m - 12) + 1, jnp.where(m >= 8, 3 * (m - 8) + 2, -9999))
        s["sel"][k, 0] = jnp.where(f == first, 1.0, 0.0).astype(BF)
        s["sel"][k, 1] = jnp.where(f == second, 1.0, 0.0).astype(BF)

    def halo_ready():
        wait(s["kw"].at[:, pl.ds(0, REACH)], s["s_halo_r"].at[0])
        wait(s["vw"].at[pl.ds(0, REACH)], s["s_halo_r"].at[1])
        wait(s["segh"], s["s_halo_r"].at[2])
        local[2].wait()
        local[3].wait()

    def seg_row(r):
        return s["segh"][4 + r : 5 + r, :] if r < 4 else seg[r - 4 : r - 3, :]

    def forward(b):
        seg_cols = jnp.transpose(seg[...].astype(F32)).astype(jnp.int32)
        seg_q = jnp.concatenate([seg_cols[:, 2 * b : 2 * b + 1], seg_cols[:, 2 * b + 1 : 2 * b + 2]], axis=0)
        pos_q = lax.broadcasted_iota(jnp.int32, (QB, 128), 0) + REACH
        pos_k = lax.broadcasted_iota(jnp.int32, (QB, 128), 1)
        scores = dot_nn(jnp.transpose(qt[:, pl.ds(QB * b, QB)]), s["kw"][:, pl.ds(QB * b, WIN)]) * SCALE
        pieces = []
        for t in range(WIN // 128):
            allowed = (seg_q == seg_row(2 * b + t)) & (pos_k + 128 * t <= pos_q)
            if 2 * b + t < 4:
                allowed = allowed & (ctx > 0)
            pieces.append(jnp.where(allowed, scores[:, 128 * t : 128 * t + 128], MASKED))
        scores = jnp.concatenate(pieces, axis=1)
        top = jnp.max(scores, axis=1, keepdims=True)
        raw = jnp.exp(scores - top)
        probs = raw / jnp.sum(raw, axis=1, keepdims=True)
        low = probs.astype(BF)
        s["probs"][b] = probs
        s["plt"][b] = jnp.transpose(low)
        s["att"][pl.ds(QB * b, QB), :] = (
            dot_nn(low, s["vw"][pl.ds(QB * b, WIN), :]).astype(BF).astype(F32)
        )

    def op_pass():
        wait(s["opf"].at[0, pl.ds(0, 64)], s["s_op_r"].at[0])
        other = lmate[1]
        for dev in xmates:
            send(s["opf"].at[other, half], s["opf"].at[other, half], s["s_op_s"], s["s_op_r"].at[2], dev)
        send(s["opf"].at[other, half], s["opf"].at[other, half], s["s_op_s"], s["s_op_r"].at[3], sibling)

    def op_cross(k, parity):
        wait(s["opf"].at[pl.ds(0, 3), pl.ds(0, 64)], s["s_op_r"].at[k])
        for step in (1, 2, 3):
            e = 2 * ((x + step) % 4) + parity
            send(s["opf"].at[e, half], s["opf"].at[e, half], s["s_op_s"], s["s_op_r"].at[3], sibling)

    def arrive(d, k, way):
        hh = (h + k) % NH
        yy = (y + NY - way * d) % NY
        j = at(hh, yy)
        src = s["w"].at[j]
        if d == 4 and k == 1:
            for part in range(2):
                wait(s["w"].at[0, pl.ds(0, 48)], s["s_half"].at[part])
        else:
            wait(s["w"].at[0], s["s_w"].at[hh * NY + yy])
        if d == 0:
            wsend(src, hh, yy, up)
            wsend(src, hh, yy, down)
        elif d < 3 or (d == 3 and k != 1 and (k == 0) == (way == 1)):
            wsend(src, hh, yy, up if way == 1 else down)
        elif d == 3 and k == 1:
            part = 0 if way == 1 else 1
            rows = pl.ds(48 * part, 48)
            send(src.at[rows], s["w"].at[j, rows], s["s_wsend"], s["s_half"].at[part], up if way == 1 else down)
        cross(src, hh, yy)

    def far_send():
        wait(s["w"].at[0], s["s_z"].at[0])
        wait(s["w"].at[0], s["s_z"].at[1])
        wsend(w_in, h, y, zs[1])
        send(op_in.at[half], s["opf"].at[me, half], s["s_op_s"], s["s_op_r"].at[0], lmate)

    def halo_send():
        send(keys_in.at[:, pl.ds(REACH, REACH)], s["kw"].at[:, pl.ds(0, REACH)],
             s["s_halo_s"].at[0], s["s_halo_r"].at[0], after)
        send(values_in.at[pl.ds(REACH, REACH)], s["vw"].at[pl.ds(0, REACH)],
             s["s_halo_s"].at[1], s["s_halo_r"].at[1], after)
        send(seg, s["segh"], s["s_halo_s"].at[2], s["s_halo_r"].at[2], after)


    def experts(k):
        hh = (h + k) % NH
        wait(s["w"].at[pl.ds(0, NY)], s["s_cross"].at[hh])
        block = pl.ds(16 * hh, 16)
        cols = pl.ds(pl.multiple_of(512 * hh, 512), 512)
        xr, w = s["xr"], s["w"]

        def stacked(first, columns):
            lead = xr[:, first : first + 16, columns].reshape(128, -1)
            tail = xr[:, 32:48, columns].reshape(128, -1)
            return jnp.concatenate([lead, tail], axis=0)

        rows_in = stacked(0, cols)
        gate = dot_nn(rows_in, w[block, 0:32, :].reshape(512, FF))
        upper = dot_nn(rows_in, w[block, 32:64, :].reshape(512, FF))
        if k == 0:
            s["pre"][:, 0:FF] = gate
            s["pre"][:, FF : 2 * FF] = upper
        else:
            s["pre"][:, 0:FF] += gate
            s["pre"][:, FF : 2 * FF] += upper
        d0 = w[block, 64:80, :].reshape(256, FF)
        d1 = w[block, 80:96, :].reshape(256, FF)
        h0 = dot_nt(stacked(16, slice(0, 768)), d0) + dot_nt(stacked(16, slice(768, 1536)), d1)
        last = stacked(16, slice(1536, 2048))
        h1 = dot_nt(last, d0[:, 0:512])
        h2 = dot_nt(last[:, 0:256], d0[:, 512:768]) + dot_nt(last[:, 256:512], d1[:, 0:256])
        h3 = dot_nt(last, d1[:, 256:768])
        m = lax.broadcasted_iota(jnp.int32, (256, 256), 1) % 16
        z1 = jnp.where(m < 12, h0, h1)
        z2 = jnp.where(m < 12, pltpu.roll(h3, 252, 1), h2)
        hid = dot_nn(z1.astype(BF), s["sel"][k, 0]) + dot_nn(z2.astype(BF), s["sel"][k, 1])
        if k == 0:
            s["hid"][...] = hid
        else:
            s["hid"][...] += hid

    normalize()
    steps = [
        (1, 0, -1), (1, 0, 1),
        lambda: dispatch(0, 512), far_send,
        (0, 1, 0), (0, 3, 0),
        lambda: dispatch(1024, 1536), dispatch_send,
        (2, 0, -1), (2, 0, 1),
        halo_send, side_send,
        (1, 1, -1), (1, 1, 1), (0, 2, 0),
        tables, lambda: selection(0),
        (1, 3, -1), (1, 3, 1),
        lambda: selection(1), clear,
        (3, 0, -1), (3, 0, 1),
        places_ready, lambda: [place_table(src) for src in range(4)],
        (2, 1, -1), (2, 1, 1),
        op_pass, lambda: [place_table(src) for src in range(4, 8)],
        (1, 2, -1), (1, 2, 1),
        halo_ready, lambda: forward(0),
        (2, 3, -1), (2, 3, 1),
        lambda: forward(1), lambda: op_cross(1, l),
        (3, 1, -1), (3, 1, 1), (4, 0, 1),
        lambda: forward(2),
        (2, 2, -1), (2, 2, 1),
        lambda: forward(3), lambda: selection(2),
        (3, 3, -1), (3, 3, 1),
        lambda: selection(3), rows_ready, lambda: experts(0),
        (3, 2, -1), (3, 2, 1),
        lambda: op_cross(2, 1 - l),
        (4, 1, 1), (4, 3, -1),
        lambda: experts(1),
        (4, 2, -1),
        lambda: experts(3), lambda: experts(2),
    ]
    for step in steps:
        if callable(step):
            step()
        else:
            arrive(*step)

    for part in range(6):
        if part < 4:
            rows = slice(32 * part, 32 * part + 32)
            gate = s["pre"][rows, 0:FF]
            upper = s["pre"][rows, FF : 2 * FF]
            hid = s["hid"][rows, :]
        else:
            rows = slice(128 + 64 * (part - 4), 192 + 64 * (part - 4))
            gate = s["pre"][rows, 0:FF].reshape(4, 16, FF)[:, 0:8].reshape(32, FF)
            upper = s["pre"][rows, FF : 2 * FF].reshape(4, 16, FF)[:, 0:8].reshape(32, FF)
            hid = s["hid"][rows, :].reshape(4, 16, FF)[:, 8:16].reshape(32, FF)
        sigm = jax.nn.sigmoid(gate)
        put = pl.ds(32 * part, 32)
        s["gg"][put, 0:FF] = (hid * upper * sigm * (1.0 + gate * (1.0 - sigm))).astype(BF)
        s["gg"][put, FF : 2 * FF] = (hid * gate * sigm).astype(BF)

    gg, os = s["gg"], s["os"]
    xr = s["xr"]
    side = jnp.concatenate(
        [s["auxr"][:, 0:16, :].reshape(128, 128), s["auxr"][:, 16:24, :].reshape(64, 128)], axis=0
    )
    inverse = side[:, 0:1] + side[:, 1:2] + side[:, 2:3]
    weight = side[:, 3:4]

    def slot_rows(first, cols):
        lead = xr[:, 16 * first : 16 * first + 16, cols].reshape(128, -1).astype(F32)
        tail = xr[:, 32:48, cols].astype(F32)[:, 8 * first : 8 * first + 8].reshape(64, -1)
        return jnp.concatenate([lead, tail], axis=0)

    dots = jnp.zeros((LIVE, 128), F32)
    for n in range(8):
        block, cols = pl.ds(8 * n, 8), pl.ds(256 * n, 256)
        grad = weight * (
            dot_nt(gg[:, 0:FF], s["w"][block, 0:32, :].reshape(256, FF))
            + dot_nt(gg[:, FF : 2 * FF], s["w"][block, 32:64, :].reshape(256, FF))
        )
        s["ng"][:, cols] = grad
        prod = grad * slot_rows(0, cols)
        dots = dots + prod[:, 0:128] + prod[:, 128:256]
    share = inverse * (jnp.sum(dots, axis=1, keepdims=True) / D)
    gain_inv = 1.0 / gain_f

    def total(n):
        cols = pl.ds(256 * n, 256)
        lanes = slice(256 * n, 256 * n + 256)
        value = (
            slot_rows(1, cols)
            + inverse * (s["ng"][:, cols] * gain_f[:, lanes])
            - slot_rows(0, cols) * share * gain_inv[:, lanes]
        )
        s["rg"][:, cols] = value.astype(BF)
        return value

    for buf in range(2):
        for sub in range(2):
            cols = pl.ds(256 * sub, 256)
            o0 = total(4 * buf + sub)
            o1 = total(4 * buf + 2 + sub)
            os[buf, :, 0:16, cols] = o0[0:128].astype(BF).reshape(N_EXP, 16, 256)
            os[buf, :, 16:32, cols] = o1[0:128].astype(BF).reshape(N_EXP, 16, 256)
            tail = jnp.concatenate(
                [o0[128:192].reshape(N_EXP, 8, 256), o1[128:192].reshape(N_EXP, 8, 256)], axis=1
            )
            os[buf, :, 32:48, cols] = tail.astype(BF)

    def home_send(buf, e):
        send(os.at[buf, e], s["orr"].at[buf, me], s["s_o"].at[buf], s["s_o"].at[2 + buf], (ctx, e))

    home_send(0, 2 * ((x + 2) % 4))
    home_send(0, 2 * ((x + 2) % 4) + 1)

    local[1].wait()
    wait(s["opf"].at[pl.ds(0, 7), pl.ds(0, 64)], s["s_op_r"].at[3])
    own_h = None
    for step in (2, 1, 3, 0):
        pair = (x + step) % 4
        proj = s["opf"][pl.ds(2 * pair, 2)].reshape(2 * VD, D)
        grads = dot_nt(s["rg"][...], proj).astype(BF)
        s["hs"][2 * pair] = grads[:, 0:VD]
        s["hs"][2 * pair + 1] = grads[:, VD : 2 * VD]
        for parity in (0, 1):
            if step:
                e = 2 * pair + parity
                send(s["hs"].at[e], s["hr"].at[me], s["s_h"].at[0], s["s_h"].at[1], (ctx, e))
        if not step:
            e = lmate[1]
            send(s["hs"].at[e], s["hr"].at[me], s["s_h"].at[0], s["s_h"].at[1], (ctx, e))
            own_h = pltpu.make_async_copy(s["hs"].at[me], s["hr"].at[me], s["s_local"].at[7])
            own_h.start()


    wait(s["hs"].at[pl.ds(0, 7)], s["s_h"].at[0])
    own_o = []
    for buf in range(2):
        for step in (2, 1, 3, 0):
            for e in (2 * ((x + step) % 4), 2 * ((x + step) % 4) + 1) if step else (lmate[1],):
                if buf or step != 2:
                    home_send(buf, e)
        copy = pltpu.make_async_copy(os.at[buf, me], s["orr"].at[buf, me], s["s_local"].at[5 + buf])
        copy.start()
        own_o.append(copy)
    own_h.wait()
    wait(s["hr"].at[pl.ds(0, 7)], s["s_h"].at[1])

    for src in range(N_EXP):
        lead = s["hr"][:, 16 * src : 16 * src + 16, :].reshape(128, VD)
        tail = s["hr"][:, 128 + 16 * (src // 2) : 144 + 16 * (src // 2), :].reshape(128, VD)
        rows = dot_nn(s["tab"][src], jnp.concatenate([lead, tail], axis=0))
        s["grads"][TOK_DEV * src : TOK_DEV * src + TOK_DEV, :] = rows.astype(BF)

    for b in range(N_QB):
        rows, window = pl.ds(QB * b, QB), pl.ds(QB * b, WIN)
        grad = s["grads"][rows, :]
        delta = jnp.sum(grad.astype(F32) * s["att"][rows, :], axis=1, keepdims=True)
        prob_grad = dot_nt(grad, s["vw"][window, :])
        score_grad = (s["probs"][b] * (prob_grad - delta)).astype(BF)
        s["dv"][window, :] += dot_nn(s["plt"][b], grad)
        s["dk"][:, window] += dot_nn(qt[:, rows], score_grad)
        out_q[:, rows] = (dot_nt(s["kw"][:, window], score_grad) * SCALE).astype(BF)
        if b < 2:
            s["ks"][b] = (s["dk"][:, rows] * SCALE).astype(BF)
            s["vs"][b] = s["dv"][rows, :].astype(BF)
            send(s["ks"].at[b], s["kr"].at[b], s["s_k"].at[b], s["s_k"].at[2 + b], before)
            send(s["vs"].at[b], s["vr"].at[b], s["s_k"].at[4 + b], s["s_k"].at[6 + b], before)
    out_k[:, 0:REACH] = (s["dk"][:, REACH : 2 * REACH] * SCALE).astype(BF)
    out_v[0:REACH, :] = s["dv"][REACH : 2 * REACH, :].astype(BF)
    for b in range(2):
        rows, mine = pl.ds(REACH + QB * b, QB), pl.ds(2 * REACH + QB * b, QB)
        wait(s["kr"].at[b], s["s_k"].at[2 + b])
        out_k[:, rows] = (s["dk"][:, mine] * SCALE + s["kr"][b].astype(F32)).astype(BF)
        wait(s["vr"].at[b], s["s_k"].at[6 + b])
        out_v[rows, :] = (s["dv"][mine, :] + s["vr"][b].astype(F32)).astype(BF)
    for buf in range(2):
        own_o[buf].wait()
        wait(s["orr"].at[buf, pl.ds(0, 7)], s["s_o"].at[2 + buf])
        got = s["orr"][buf].reshape(N_EXP * SLOTS, 512)
        out_res[:, 1024 * buf : 1024 * buf + 512] = dot_nn(s["tin"][...], got).astype(BF)
        out_res[:, 1024 * buf + 512 : 1024 * buf + 1024] = dot_nn(s["tdy"][...], got).astype(BF)

    wait(s["w"].at[pl.ds(0, 61)], s["s_wsend"])
    wait(s["opf"].at[pl.ds(0, 7)], s["s_op_s"])
    wait(keys_in.at[:, pl.ds(0, REACH)], s["s_halo_s"].at[0])
    wait(values_in.at[pl.ds(0, REACH)], s["s_halo_s"].at[1])
    wait(s["segh"], s["s_halo_s"].at[2])
    wait(s["xs"].at[pl.ds(0, 7)], s["s_x"].at[0])
    wait(s["auxs"].at[pl.ds(0, 7)], s["s_aux"].at[0])
    wait(s["placer"].at[pl.ds(0, 7)], s["s_aux"].at[2])
    for buf in range(2):
        wait(os.at[buf, pl.ds(0, 7)], s["s_o"].at[buf])
    for b in range(2):
        wait(s["ks"].at[b], s["s_k"].at[b])
        wait(s["vs"].at[b], s["s_k"].at[4 + b])


def hand_over(a, b, c, d, oa, ob, oc, od, va, vb, vc, vd, sem):
    triples = ((a, va, oa), (b, vb, ob), (c, vc, oc), (d, vd, od))
    into = [pltpu.make_async_copy(t[0], t[1], sem.at[i]) for i, t in enumerate(triples)]
    out = [pltpu.make_async_copy(t[1], t[2], sem.at[4 + i]) for i, t in enumerate(triples)]
    for copy in into:
        copy.start()
    for i in range(4):
        into[i].wait()
        out[i].start()
    for copy in out:
        copy.wait()


def shards(
    residual, out_grad, norm_gain, expert_ids, route_weights, gate_up, down_proj, out_proj,
    queries, keys_in, values_in, segments,
):
    vm = pl.BlockSpec(memory_space=pltpu.VMEM)
    hbm = pl.BlockSpec(memory_space=pl.ANY)
    results = pl.pallas_call(
        body,
        out_shape=(
            jax.ShapeDtypeStruct((TOK_DEV, D), BF),
            jax.ShapeDtypeStruct((QK, TOK), BF),
            jax.ShapeDtypeStruct((QK, TOK), BF),
            jax.ShapeDtypeStruct((TOK, VD), BF),
        ),
        in_specs=[hbm] * 4 + [vm] * 8,
        out_specs=(vm,) * 4,
        scratch_shapes=list(scratch().values()),
        compiler_params=pltpu.CompilerParams(
            collective_id=0, has_side_effects=True, vmem_limit_bytes=60 * 1024 * 1024
        ),
    )(
        gate_up.reshape(64, FF), out_proj, keys_in.T, values_in, down_proj.reshape(12, D),
        residual, out_grad, norm_gain.reshape(16, 128), expert_ids.T, route_weights.T,
        segments.reshape(8, 128), queries.T,
    )
    residual_grad, query_grad, key_grad, value_grad = pl.pallas_call(
        hand_over,
        out_shape=tuple(jax.ShapeDtypeStruct(r.shape, r.dtype) for r in results),
        in_specs=[hbm] * 4,
        out_specs=(hbm,) * 4,
        scratch_shapes=[pltpu.VMEM(r.shape, r.dtype) for r in results] + [pltpu.SemaphoreType.DMA((8,))],
    )(*results)
    return residual_grad, query_grad.T, key_grad.T, value_grad


def solution(mesh):
    return jax.shard_map(
        shards,
        mesh=mesh,
        in_specs=(
            P(("ctx", "exp"), None),
            P(("ctx", "exp"), None),
            P(),
            P(("ctx", "exp"), None),
            P(("ctx", "exp"), None),
            P("exp", None, "ctx", None),
            P("exp", "ctx", None),
            P("exp", None),
            P("ctx", "exp"),
            P("ctx", "exp"),
            P("ctx", "exp"),
            P("ctx"),
        ),
        out_specs=(P(("ctx", "exp"), None), P("ctx", "exp"), P("ctx", "exp"), P("ctx", "exp")),
        check_vma=False,
    )
```
